32 devices in a mesh: shot: 2 (over x), chan: 16 (over z, y, core).
Axes of the slice: x: 2, y: 2, z: 4, core: 2. Of those that a mesh axis runs over, the one named last changes fastest.
Arguments:
- traces: float32 [8, 256, 4096], P('shot', 'chan'), may hold values from -6 to 6
- shifts: int32 [8, 256], P('shot', 'chan'), may hold values from 0 to 1023
- aperture_lo: int32 [256], P('chan'), may hold values from 0 to 3
- aperture_hi: int32 [256], P('chan'), may hold values from 5 to 8
- dip_band: int32 [256], P('chan'), may hold values from 64 to 512
Outputs:
- filtered: float32 [8, 256, 4096], P(None, ('chan', 'shot'))
The draws below stay inside these ranges and needn't reach their ends.
All inputs are finite; a program needn't handle non-finite values.
Results may differ from the reference program's by a relative error of at most 0.0003.
Values sent between devices are 32-bit elements; how exact they have to be, the bound alone decides.
A program may use at most 64 MiB of HBM per device.

```python
import jax
import jax.numpy as jnp
from jax import lax

CH_DEV = 16
NT = 4096
SHOTS = 8
CHANNELS = 256


def place_ends(entries, stream_key, smallest, top_value):
    longest = entries.shape.index(max(entries.shape))
    spots = []
    for shift in (0, 1):
        where = [jax.random.randint(jax.random.fold_in(stream_key, axis), (), 0, length) for axis, length in enumerate(entries.shape)]
        where[longest] = (where[longest] + shift) % entries.shape[longest]
        spots.append(tuple(where))
    return entries.at[spots[0]].set(smallest).at[spots[1]].set(top_value)


def levels(stream_key, shape, cuts, low, top_value):
    def one(position, parts):
        heights = jax.random.uniform(jax.random.fold_in(jax.random.fold_in(stream_key, 6), position), (parts,), jnp.float32, low / len(cuts), top_value / len(cuts))
        return jnp.repeat(jnp.exp(heights), shape[position] // parts).reshape((-1,) + (1,) * (len(shape) - position - 1))

    factor_of = one(*cuts[0])
    for cut in cuts[1:]:
        factor_of = factor_of * one(*cut)
    return factor_of


def bell_draw(key, shape, scale, most, cuts=(), kind=jnp.bfloat16):
    values = jax.random.normal(key, shape, jnp.float32) * scale
    if len(cuts) > 0:
        values = levels(key, shape, cuts, -0.22, 0.18) * values
    return jnp.clip(values, min=-most, max=most).astype(kind)


def setup_inputs(seed: int = 0) -> dict:
    splits = jax.random.split(jax.random.key(seed), 6)
    return {
        "traces": bell_draw(splits[0], (SHOTS, CHANNELS, NT), 1.0, 6.0, ((0, 2), (1, 16)), jnp.float32),
        "shifts": place_ends(jax.random.randint(splits[1], (SHOTS, CHANNELS), 0, NT // 4), jax.random.fold_in(splits[1], 1), 0, (NT // 4) - 1).astype(jnp.int32),
        "aperture_lo": place_ends(jax.random.randint(splits[2], (CHANNELS,), 0, SHOTS // 2), jax.random.fold_in(splits[2], 1), 0, (SHOTS // 2) - 1).astype(jnp.int32),
        "aperture_hi": place_ends(jax.random.randint(splits[3], (CHANNELS,), SHOTS // 2 + 1, SHOTS + 1), jax.random.fold_in(splits[3], 1), SHOTS // 2 + 1, SHOTS).astype(jnp.int32),
        "dip_band": place_ends(jax.random.randint(splits[4], (CHANNELS,), NT // 64, NT // 8 + 1), jax.random.fold_in(splits[4], 1), NT // 64, (NT // 8 + 1) - 1).astype(jnp.int32),
    }


def median_channels(signal):
    padded = jnp.pad(signal, ((5, 5), (0, 0)))
    count = signal.shape[0]
    stacked = jnp.stack([padded[offset:offset + count] for offset in range(11)])
    return jnp.sort(stacked, axis=0)[5]


def clean_shot(packed):
    trace_block, shift_row = packed
    samples_ids = jnp.arange(NT, dtype=jnp.int32)
    source = samples_ids[None, :] + shift_row[:, None]
    picked = jnp.take_along_axis(trace_block, jnp.minimum(source, NT - 1).astype(jnp.int32), axis=1)
    aligned = jnp.where(source < NT, picked, jnp.zeros_like(picked))
    first_pass = aligned - median_channels(aligned)
    second_pass = first_pass - median_channels(first_pass)
    backward = samples_ids[None, :] - shift_row[:, None]
    picked_back = jnp.take_along_axis(second_pass, jnp.maximum(backward, 0).astype(jnp.int32), axis=1)
    return jnp.where(backward >= 0, picked_back, jnp.zeros_like(picked_back))


def reference(traces, shifts, aperture_lo, aperture_hi, dip_band):
    upgoing = lax.map(clean_shot, (traces, shifts))
    shot_ids = jnp.arange(SHOTS, dtype=jnp.int32)
    in_aperture = (shot_ids[:, None] >= aperture_lo[None, :]) & (shot_ids[:, None] < aperture_hi[None, :])
    upgoing = jnp.where(in_aperture[:, :, None], upgoing, jnp.zeros_like(upgoing))
    wave_ids = jnp.arange(SHOTS, dtype=jnp.int32)
    wave_abs = jnp.abs(jnp.where(wave_ids < SHOTS // 2, wave_ids, wave_ids - SHOTS))
    freq_ids = jnp.arange(NT, dtype=jnp.int32)
    freq_abs = jnp.abs(jnp.where(freq_ids < NT // 2, freq_ids, freq_ids - NT))
    block_count = CHANNELS // CH_DEV
    grouped = upgoing.reshape(SHOTS, block_count, CH_DEV, NT).transpose(1, 0, 2, 3)
    band_blocks = dip_band.reshape(block_count, CH_DEV)

    def filter_group(packed):
        gathered, band_rows = packed
        spectrum = jnp.fft.fft2(gathered, axes=(0, 2))
        pass_mask = (wave_abs[:, None, None] * band_rows[None, :, None]) <= freq_abs[None, None, :]
        spectrum = jnp.where(pass_mask, spectrum, jnp.zeros_like(spectrum))
        return jnp.real(jnp.fft.ifft2(spectrum, axes=(0, 2)))

    result = lax.map(filter_group, (grouped, band_blocks))
    return result.transpose(1, 0, 2, 3).reshape(SHOTS, CHANNELS, NT)
```

```python
import functools
import math

import jax
import jax.numpy as jnp
import numpy as np
from jax import lax
from jax.experimental import pallas as pl
from jax.experimental.pallas import tpu as pltpu
from jax.sharding import PartitionSpec as P

LANES = 128
REACH = 5
HALO = 2 * REACH


def sort_two(a, b):
    return jnp.minimum(a, b), jnp.maximum(a, b)


def median_rows(rows, centers):
    pairs = {}
    fours = {}
    results = {}

    def pair(at):
        if at not in pairs:
            pairs[at] = sort_two(rows[at], rows[at + 1])
        return pairs[at]

    def four(at):
        if at not in fours:
            a, b = pair(at)
            c, d = pair(at + 2)
            low, mid_a = sort_two(a, c)
            mid_b, high = sort_two(b, d)
            mid_a, mid_b = sort_two(mid_a, mid_b)
            fours[at] = (low, mid_a, mid_b, high)
        return fours[at]

    def middle_two(core, extra):
        a, b, c, d = core
        p, q = extra
        low = jnp.minimum(c, jnp.minimum(jnp.maximum(b, p), jnp.maximum(a, q)))
        high = jnp.maximum(b, jnp.maximum(jnp.minimum(d, p), jnp.minimum(c, q)))
        return low, high

    def clamp(value, ends):
        return jnp.maximum(ends[0], jnp.minimum(value, ends[1]))

    last = centers[-1]
    for c in centers[::4]:
        x, y = four(c - 2), four(c + 2)
        low = [jnp.minimum(x[i], y[3 - i]) for i in range(4)]
        high = [jnp.maximum(x[i], y[3 - i]) for i in range(4)]
        core = sort_two(jnp.maximum(low[0], low[2]), jnp.maximum(low[1], low[3])) + sort_two(
            jnp.minimum(high[0], high[2]), jnp.minimum(high[1], high[3])
        )
        ends = middle_two(core, pair(c - 4))
        results[c] = clamp(rows[c - 5], ends)
        results[c + 1] = clamp(rows[c + 6], ends)
        if c + 2 <= last:
            ends = middle_two(core, pair(c + 6))
            results[c + 2] = clamp(rows[c - 3], ends)
            results[c + 3] = clamp(rows[c + 8], ends)
    return results


def turn(value, angle_index, size, sign):
    re, im = value
    angle_index = angle_index % size
    if angle_index == 0:
        return value
    if 4 * angle_index == size:
        return (-im, re) if sign > 0 else (im, -re)
    if 2 * angle_index == size:
        return (-re, -im)
    angle = 2.0 * math.pi * angle_index / size
    cos, sin = math.cos(angle), sign * math.sin(angle)
    if 8 * angle_index == size:
        return ((re - im) * cos, (re + im) * cos) if sign > 0 else ((re + im) * cos, (im - re) * cos)
    return (re * cos - im * sin, re * sin + im * cos)


def add(a, b):
    return (a[0] + b[0], a[1] + b[1])


def sub(a, b):
    return (a[0] - b[0], a[1] - b[1])


def conj(a):
    return (a[0], -a[1])


def complex_dft(values, sign):
    size = len(values)
    if size == 1:
        return values
    even = complex_dft(values[0::2], sign)
    odd = complex_dft(values[1::2], sign)
    odd = [turn(odd[k], k, size, sign) for k in range(size // 2)]
    return [add(even[k], odd[k]) for k in range(size // 2)] + [
        sub(even[k], odd[k]) for k in range(size // 2)
    ]


def real_dft(values):
    size = len(values)
    if size == 2:
        zero = jnp.zeros_like(values[0])
        return [(values[0] + values[1], zero), (values[0] - values[1], zero)]
    even, odd = real_dft(values[0::2]), real_dft(values[1::2])
    half = size // 2
    zero = jnp.zeros_like(values[0])
    result = [None] * (half + 1)
    result[0] = (even[0][0] + odd[0][0], zero)
    result[half] = (even[0][0] - odd[0][0], zero)
    for k in range(1, half // 2 + 1):
        if 2 * k == half:
            result[k] = (even[k][0], -odd[k][0])
        else:
            moved = turn(odd[k], k, size, -1)
            result[k] = add(even[k], moved)
            result[half - k] = conj(sub(even[k], moved))
    return result


def real_inverse(values, size):
    half = size // 2
    if size == 2:
        a, b = values[0][0], values[1][0]
        return [a + b, a - b]
    even, odd = [], []
    for k in range(half // 2 + 1):
        if k == 0:
            even.append((values[0][0] + values[half][0], None))
            odd.append((values[0][0] - values[half][0], None))
        elif 2 * k == half:
            even.append((2.0 * values[k][0], None))
            odd.append((-2.0 * values[k][1], None))
        else:
            other = conj(values[half - k])
            even.append(add(values[k], other))
            odd.append(turn(sub(values[k], other), k, size, 1))
    first, second = real_inverse(even, half), real_inverse(odd, half)
    return [item for both in zip(first, second) for item in both]


def split_dot(x, high_table, low_table):
    high = x.astype(jnp.bfloat16)
    low = (x - high.astype(jnp.float32)).astype(jnp.bfloat16)

    def dot(a, b):
        return jnp.dot(a, b, preferred_element_type=jnp.float32)

    return dot(high, high_table) + (dot(low, high_table) + dot(high, low_table))


def to_sublanes(row, count, start):
    size = row.shape[1]
    row_ids = lax.broadcasted_iota(jnp.int32, (count, size), 0)
    col_ids = lax.broadcasted_iota(jnp.int32, (count, size), 1)
    spread = jnp.broadcast_to(row.astype(jnp.float32), (count, size))
    picked = jnp.where(col_ids == row_ids + start, spread, 0.0)
    return jnp.sum(picked, axis=1, keepdims=True).astype(jnp.int32)


def kernel(
    groups, blocks,
    traces, shifts, lo_ref, hi_ref, band_ref, fwd_hi, fwd_lo, inv_hi, inv_lo, twist,
    out,
    ext, second, up, got, spec,
    halo_send, halo_recv, part_send, part_recv,
):
    shot_local, chan_local, length = traces.shape
    outer = length // LANES
    half = outer // 2 + 1
    rec = chan_local // groups
    shots = groups * shot_local
    ext_rows = (chan_local + 2 * HALO) * outer
    halo_rows = HALO * outer
    part = lax.axis_index("shot")
    block = lax.axis_index("chan")
    mesh_id = pl.DeviceIdType.MESH
    has_left = block > 0
    has_right = block < blocks - 1
    left = jnp.maximum(block - 1, 0)
    right = jnp.minimum(block + 1, blocks - 1)
    q_bits = max((length // 4 // LANES - 1).bit_length(), 0)

    barrier = pltpu.get_barrier_semaphore()

    @pl.when(has_left)
    def _():
        pl.semaphore_signal(barrier, inc=1, device_id=(part, left), device_id_type=mesh_id)

    @pl.when(has_right)
    def _():
        pl.semaphore_signal(barrier, inc=1, device_id=(part, right), device_id_type=mesh_id)

    for offset in range(1, groups):
        pl.semaphore_signal(
            barrier, inc=1, device_id=(lax.rem(part + offset, groups), block), device_id_type=mesh_id
        )

    def rotate_index(column, sign, rows):
        lanes = lax.broadcasted_iota(jnp.int32, (rows, LANES), 1)
        low = jnp.broadcast_to(column & (LANES - 1), (rows, LANES))
        if sign > 0:
            place = lanes + low
            return place & (LANES - 1), place >= LANES
        place = lanes - low
        return place & (LANES - 1), place < 0

    def move(chunks, column, sign, rows):
        index, crossed = rotate_index(column, sign, rows)
        zero = jnp.zeros((rows, LANES), jnp.float32)
        turned = [jnp.take_along_axis(chunk, index, axis=1) for chunk in chunks]

        def at(items, place):
            return items[place] if 0 <= place < outer else zero

        moved = [jnp.where(crossed, at(turned, a + sign), turned[a]) for a in range(outer)]
        for bit in range(q_bits):
            chosen = jnp.broadcast_to((column >> (7 + bit)) & 1, (rows, LANES)) == 1
            stride = sign << bit if sign > 0 else -(1 << bit)
            moved = [jnp.where(chosen, at(moved, a + stride), moved[a]) for a in range(outer)]
        return moved

    def halo_copies(s):
        base = pl.multiple_of(s * ext_rows, 8)
        to_right = pltpu.make_async_remote_copy(
            src_ref=ext.at[pl.ds(base + chan_local * outer, halo_rows)],
            dst_ref=ext.at[pl.ds(base, halo_rows)],
            send_sem=halo_send.at[s, 0],
            recv_sem=halo_recv.at[s, 0],
            device_id=(part, right),
            device_id_type=mesh_id,
        )
        to_left = pltpu.make_async_remote_copy(
            src_ref=ext.at[pl.ds(base + halo_rows, halo_rows)],
            dst_ref=ext.at[pl.ds(base + halo_rows + chan_local * outer, halo_rows)],
            send_sem=halo_send.at[s, 1],
            recv_sem=halo_recv.at[s, 1],
            device_id=(part, left),
            device_id_type=mesh_id,
        )
        return to_right, to_left

    def part_copy(s, offset):
        other = lax.rem(part + offset, groups)
        return pltpu.make_async_remote_copy(
            src_ref=up.at[s, other],
            dst_ref=got.at[part * shot_local + s],
            send_sem=part_send.at[s, offset - 1],
            recv_sem=part_recv.at[s, offset - 1],
            device_id=(other, block),
            device_id_type=mesh_id,
        )

    def align(s):
        row = shifts[pl.ds(s, 1), :]
        for top in range(0, chan_local, 8):
            column = to_sublanes(row, 8, top)
            chunks = [traces[s, top : top + 8, a * LANES : (a + 1) * LANES] for a in range(outer)]
            moved = move(chunks, column, 1, 8)
            for a in range(outer):
                start = s * ext_rows + (HALO + top) * outer + a
                ext[pl.ds(start, 8, stride=outer), :] = moved[a]

    def send_halos(s):
        to_right, to_left = halo_copies(s)

        @pl.when(has_right)
        def _():
            to_right.start()

        @pl.when(has_left)
        def _():
            to_left.start()

    align(0)
    expected = has_left.astype(jnp.int32) + has_right.astype(jnp.int32) + (groups - 1)
    pl.semaphore_wait(barrier, expected)
    send_halos(0)

    def align_step(s, carry):
        align(s)
        send_halos(s)
        return carry

    lax.fori_loop(1, shot_local, align_step, 0)

    @pl.when(jnp.logical_not(has_left))
    def _():
        for s in range(shot_local):
            ext[s * ext_rows : s * ext_rows + halo_rows, :] = jnp.zeros((halo_rows, LANES), jnp.float32)

    @pl.when(jnp.logical_not(has_right))
    def _():
        for s in range(shot_local):
            ext[(s + 1) * ext_rows - halo_rows : (s + 1) * ext_rows, :] = jnp.zeros(
                (halo_rows, LANES), jnp.float32
            )

    def forward(load, shot_id):
        values = real_dft([load(a) for a in range(outer)])
        for c in range(half):
            re, im = values[c]
            cos, sin = twist[0, c : c + 1, :], twist[1, c : c + 1, :]
            spec[shot_id, c, :, 0:LANES] = re * cos + im * sin
            spec[shot_id, c, :, LANES : 2 * LANES] = im * cos - re * sin
        padded = spec.shape[1]
        if padded > half:
            spec[shot_id, half:padded] = jnp.zeros((padded - half, rec, 2 * LANES), jnp.float32)
        flat = spec[shot_id].reshape(padded * rec, 2 * LANES)
        flat = split_dot(flat, fwd_hi[...], fwd_lo[...])
        spec[shot_id] = flat.reshape(padded, rec, 2 * LANES)

    edge_low = jnp.broadcast_to(has_left, (8, LANES))
    edge_high = jnp.broadcast_to(has_right, (8, LANES))

    def clean_step(s, carry):
        to_right, to_left = halo_copies(s)

        @pl.when(has_left)
        def _():
            to_right.wait_recv()

        @pl.when(has_right)
        def _():
            to_left.wait_recv()

        base = s * ext_rows

        def median_step(tile, carry):
            def rows_at(j):
                return ext[pl.ds(pl.multiple_of(base + j * outer + tile * 8, 8), 8), :]

            rows = {j: rows_at(j) for j in range(chan_local + 2 * HALO)}
            centers = list(range(REACH, chan_local + 2 * HALO - REACH))
            found = median_rows(rows, centers)
            cleaned = {}
            for j in centers:
                value = rows[j] - found[j]
                if j < HALO:
                    value = jnp.where(edge_low, value, 0.0)
                elif j >= HALO + chan_local:
                    value = jnp.where(edge_high, value, 0.0)
                cleaned[j] = value
            centers = list(range(HALO, HALO + chan_local))
            found = median_rows(cleaned, centers)
            for j in centers:
                start = pl.multiple_of((j - HALO) * outer + tile * 8, 8)
                second[pl.ds(start, 8), :] = cleaned[j] - found[j]
            return carry

        lax.fori_loop(0, outer // 8, median_step, 0)

        shot_id = part * shot_local + s
        row = shifts[pl.ds(s, 1), :]
        for g in range(groups):
            column = to_sublanes(row, rec, g * rec)
            low = to_sublanes(lo_ref[...], rec, g * rec)
            high = to_sublanes(hi_ref[...], rec, g * rec)
            inside = jnp.broadcast_to(((low <= shot_id) & (high > shot_id)).astype(jnp.int32), (rec, LANES)) == 1
            chunks = [
                second[pl.ds(g * rec * outer + a, rec, stride=outer), :] for a in range(outer)
            ]
            moved = move(chunks, column, -1, rec)
            for a in range(outer):
                up[s, g, a] = jnp.where(inside, moved[a], 0.0)
        for offset in range(1, groups):
            part_copy(s, offset).start()
        forward(lambda a: up[s, part, a], shot_id)
        return carry

    lax.fori_loop(0, shot_local, clean_step, 0)

    def arrive_step(s, carry):
        for offset in range(1, groups):
            part_copy(s, offset).wait_recv()
            source = lax.rem(part + groups - offset, groups)
            shot_id = source * shot_local + s
            forward(lambda a: got[shot_id, a], shot_id)
        return carry

    lax.fori_loop(0, shot_local, arrive_step, 0)

    band = jnp.broadcast_to(to_sublanes(band_ref[...], rec, part * rec), (rec, LANES))
    lane_ids = lax.broadcasted_iota(jnp.int32, (rec, LANES), 1)

    def dip_step(c, carry):
        frequency = lane_ids * outer + c
        freq_abs = jnp.minimum(frequency, length - frequency)
        values = [
            (spec[s, c, :, 0:LANES], spec[s, c, :, LANES : 2 * LANES]) for s in range(shots)
        ]
        waves = complex_dft(values, -1)
        kept = []
        for k in range(shots):
            keep = min(k, shots - k) * band <= freq_abs
            kept.append((jnp.where(keep, waves[k][0], 0.0), jnp.where(keep, waves[k][1], 0.0)))
        values = complex_dft(kept, 1)
        for s in range(shots):
            spec[s, c, :, 0:LANES] = values[s][0]
            spec[s, c, :, LANES : 2 * LANES] = values[s][1]
        return carry

    lax.fori_loop(0, half, dip_step, 0)

    def back_step(s, carry):
        padded = spec.shape[1]
        flat = spec[s].reshape(padded * rec, 2 * LANES)
        flat = split_dot(flat, inv_hi[...], inv_lo[...])
        spec[s] = flat.reshape(padded, rec, 2 * LANES)
        values = []
        for c in range(half):
            re, im = spec[s, c, :, 0:LANES], spec[s, c, :, LANES : 2 * LANES]
            cos, sin = twist[0, c : c + 1, :], twist[1, c : c + 1, :]
            values.append((re * cos - im * sin, im * cos + re * sin))
        for a, value in enumerate(real_inverse(values, outer)):
            out[s, :, a * LANES : (a + 1) * LANES] = value
        return carry

    lax.fori_loop(0, shots, back_step, 0)

    def drain_step(s, carry):
        to_right, to_left = halo_copies(s)

        @pl.when(has_right)
        def _():
            to_right.wait_send()

        @pl.when(has_left)
        def _():
            to_left.wait_send()

        for offset in range(1, groups):
            part_copy(s, offset).wait_send()
        return carry

    lax.fori_loop(0, shot_local, drain_step, 0)


def halves(table):
    high = table.astype(jnp.bfloat16)
    return high, (table - high.astype(np.float64)).astype(jnp.bfloat16)


def tables(shots, length):
    outer = length // LANES
    ids = np.arange(LANES)
    angles = 2.0 * np.pi * (np.outer(ids, ids) % LANES) / LANES
    cos, sin = np.cos(angles), np.sin(angles)
    forward = np.block([[cos, -sin], [sin, cos]])
    inverse = np.block([[cos, sin], [-sin, cos]]) / (shots * length)
    product = np.outer(np.arange(outer // 2 + 1), ids) % length
    angles = 2.0 * np.pi * product / length
    twist = np.stack([np.cos(angles), np.sin(angles)]).astype(np.float32)
    return halves(forward) + halves(inverse) + (twist,)


def local(groups, blocks, traces, shifts, aperture_lo, aperture_hi, dip_band):
    shot_local, chan_local, length = traces.shape
    outer = length // LANES
    rec = chan_local // groups
    shots = groups * shot_local
    padded = outer // 2 + 2
    constants = [jnp.asarray(table) for table in tables(shots, length)]
    vmem = pl.BlockSpec(memory_space=pltpu.VMEM)
    others = max(groups - 1, 1)
    return pl.pallas_call(
        functools.partial(kernel, groups, blocks),
        out_shape=jax.ShapeDtypeStruct((shots, rec, length), jnp.float32),
        in_specs=[vmem] * 10,
        out_specs=vmem,
        scratch_shapes=[
            pltpu.VMEM((shot_local * (chan_local + 2 * HALO) * outer, LANES), jnp.float32),
            pltpu.VMEM((chan_local * outer, LANES), jnp.float32),
            pltpu.VMEM((shot_local, groups, outer, rec, LANES), jnp.float32),
            pltpu.VMEM((shots, outer, rec, LANES), jnp.float32),
            pltpu.VMEM((shots, padded, rec, 2 * LANES), jnp.float32),
            pltpu.SemaphoreType.DMA((shot_local, 2)),
            pltpu.SemaphoreType.DMA((shot_local, 2)),
            pltpu.SemaphoreType.DMA((shot_local, others)),
            pltpu.SemaphoreType.DMA((shot_local, others)),
        ],
        compiler_params=pltpu.CompilerParams(
            collective_id=0, has_side_effects=True, vmem_limit_bytes=48 * 1024 * 1024
        ),
    )(
        traces, shifts, aperture_lo[None, :], aperture_hi[None, :], dip_band[None, :], *constants
    )


def solution(mesh):
    return jax.shard_map(
        functools.partial(local, mesh.shape["shot"], mesh.shape["chan"]),
        mesh=mesh,
        in_specs=(P("shot", "chan", None), P("shot", "chan"), P("chan"), P("chan"), P("chan")),
        out_specs=P(None, ("chan", "shot"), None),
        check_vma=False,
    )
```

```python
import functools
import math

import jax
import jax.numpy as jnp
import numpy as np
from jax import lax
from jax.experimental import pallas as pl
from jax.experimental.pallas import tpu as pltpu
from jax.sharding import PartitionSpec as P

LANES = 128
REACH = 5
HALO = 2 * REACH


def sort_two(a, b):
    return jnp.minimum(a, b), jnp.maximum(a, b)


def median_rows(rows, centers):
    pairs = {}
    fours = {}
    results = {}

    def pair(at):
        if at not in pairs:
            pairs[at] = sort_two(rows[at], rows[at + 1])
        return pairs[at]

    def four(at):
        if at not in fours:
            a, b = pair(at)
            c, d = pair(at + 2)
            low, mid_a = sort_two(a, c)
            mid_b, high = sort_two(b, d)
            mid_a, mid_b = sort_two(mid_a, mid_b)
            fours[at] = (low, mid_a, mid_b, high)
        return fours[at]

    def middle_two(core, extra):
        a, b, c, d = core
        p, q = extra
        low = jnp.minimum(c, jnp.minimum(jnp.maximum(b, p), jnp.maximum(a, q)))
        high = jnp.maximum(b, jnp.maximum(jnp.minimum(d, p), jnp.minimum(c, q)))
        return low, high

    def clamp(value, ends):
        return jnp.maximum(ends[0], jnp.minimum(value, ends[1]))

    last = centers[-1]
    for c in centers[::4]:
        x, y = four(c - 2), four(c + 2)
        low = [jnp.minimum(x[i], y[3 - i]) for i in range(4)]
        high = [jnp.maximum(x[i], y[3 - i]) for i in range(4)]
        core = sort_two(jnp.maximum(low[0], low[2]), jnp.maximum(low[1], low[3])) + sort_two(
            jnp.minimum(high[0], high[2]), jnp.minimum(high[1], high[3])
        )
        ends = middle_two(core, pair(c - 4))
        results[c] = clamp(rows[c - 5], ends)
        results[c + 1] = clamp(rows[c + 6], ends)
        if c + 2 <= last:
            ends = middle_two(core, pair(c + 6))
            results[c + 2] = clamp(rows[c - 3], ends)
            results[c + 3] = clamp(rows[c + 8], ends)
    return results


def turn(value, angle_index, size, sign):
    re, im = value
    angle_index = angle_index % size
    if angle_index == 0:
        return value
    if 4 * angle_index == size:
        return (-im, re) if sign > 0 else (im, -re)
    if 2 * angle_index == size:
        return (-re, -im)
    angle = 2.0 * math.pi * angle_index / size
    cos, sin = math.cos(angle), sign * math.sin(angle)
    if 8 * angle_index == size:
        return ((re - im) * cos, (re + im) * cos) if sign > 0 else ((re + im) * cos, (im - re) * cos)
    return (re * cos - im * sin, re * sin + im * cos)


def add(a, b):
    return (a[0] + b[0], a[1] + b[1])


def sub(a, b):
    return (a[0] - b[0], a[1] - b[1])


def conj(a):
    return (a[0], -a[1])


def complex_dft(values, sign):
    size = len(values)
    if size == 1:
        return values
    even = complex_dft(values[0::2], sign)
    odd = complex_dft(values[1::2], sign)
    odd = [turn(odd[k], k, size, sign) for k in range(size // 2)]
    return [add(even[k], odd[k]) for k in range(size // 2)] + [
        sub(even[k], odd[k]) for k in range(size // 2)
    ]


def real_dft(values):
    size = len(values)
    if size == 2:
        zero = jnp.zeros_like(values[0])
        return [(values[0] + values[1], zero), (values[0] - values[1], zero)]
    even, odd = real_dft(values[0::2]), real_dft(values[1::2])
    half = size // 2
    zero = jnp.zeros_like(values[0])
    result = [None] * (half + 1)
    result[0] = (even[0][0] + odd[0][0], zero)
    result[half] = (even[0][0] - odd[0][0], zero)
    for k in range(1, half // 2 + 1):
        if 2 * k == half:
            result[k] = (even[k][0], -odd[k][0])
        else:
            moved = turn(odd[k], k, size, -1)
            result[k] = add(even[k], moved)
            result[half - k] = conj(sub(even[k], moved))
    return result


def real_inverse(values, size):
    half = size // 2
    if size == 2:
        a, b = values[0][0], values[1][0]
        return [a + b, a - b]
    even, odd = [], []
    for k in range(half // 2 + 1):
        if k == 0:
            even.append((values[0][0] + values[half][0], None))
            odd.append((values[0][0] - values[half][0], None))
        elif 2 * k == half:
            even.append((2.0 * values[k][0], None))
            odd.append((-2.0 * values[k][1], None))
        else:
            other = conj(values[half - k])
            even.append(add(values[k], other))
            odd.append(turn(sub(values[k], other), k, size, 1))
    first, second = real_inverse(even, half), real_inverse(odd, half)
    return [item for both in zip(first, second) for item in both]


def split_dot(x, high_table, low_table):
    high = x.astype(jnp.bfloat16)
    low = (x - high.astype(jnp.float32)).astype(jnp.bfloat16)

    def dot(a, b):
        return jnp.dot(a, b, preferred_element_type=jnp.float32)

    return dot(high, high_table) + (dot(low, high_table) + dot(high, low_table))


def to_sublanes(row, count, start):
    size = row.shape[1]
    row_ids = lax.broadcasted_iota(jnp.int32, (count, size), 0)
    col_ids = lax.broadcasted_iota(jnp.int32, (count, size), 1)
    spread = jnp.broadcast_to(row.astype(jnp.float32), (count, size))
    picked = jnp.where(col_ids == row_ids + start, spread, 0.0)
    return jnp.sum(picked, axis=1, keepdims=True).astype(jnp.int32)


def kernel(
    groups, blocks,
    traces_hbm, *rest,
):
    small_hbm, (out,), scratch = rest[:9], rest[9:10], rest[10:]
    traces, small, scratch = scratch[0], scratch[1:10], scratch[10:]
    shifts, lo_ref, hi_ref, band_ref, fwd_hi, fwd_lo, inv_hi, inv_lo, twist = small
    ext, second, up, got, spec, halo_send, halo_recv, part_send, part_recv, load_sem, small_sem = scratch
    shot_local, chan_local, length = traces.shape
    outer = length // LANES
    half = outer // 2 + 1
    rec = chan_local // groups
    shots = groups * shot_local
    ext_rows = (chan_local + 2 * HALO) * outer
    halo_rows = HALO * outer
    part = lax.axis_index("shot")
    block = lax.axis_index("chan")
    mesh_id = pl.DeviceIdType.MESH
    has_left = block > 0
    has_right = block < blocks - 1
    left = jnp.maximum(block - 1, 0)
    right = jnp.minimum(block + 1, blocks - 1)
    q_bits = max((length // 4 // LANES - 1).bit_length(), 0)

    small_loads = [
        pltpu.make_async_copy(small_hbm[i], small[i], small_sem.at[i]) for i in range(len(small))
    ]
    trace_loads = [
        pltpu.make_async_copy(traces_hbm.at[s], traces.at[s], load_sem.at[s]) for s in range(shot_local)
    ]
    small_loads[0].start()
    for load in trace_loads + small_loads[1:]:
        load.start()

    barrier = pltpu.get_barrier_semaphore()

    @pl.when(has_left)
    def _():
        pl.semaphore_signal(barrier, inc=1, device_id=(part, left), device_id_type=mesh_id)

    @pl.when(has_right)
    def _():
        pl.semaphore_signal(barrier, inc=1, device_id=(part, right), device_id_type=mesh_id)

    for offset in range(1, groups):
        pl.semaphore_signal(
            barrier, inc=1, device_id=(lax.rem(part + offset, groups), block), device_id_type=mesh_id
        )

    def rotate_index(column, sign, rows):
        lanes = lax.broadcasted_iota(jnp.int32, (rows, LANES), 1)
        low = jnp.broadcast_to(column & (LANES - 1), (rows, LANES))
        if sign > 0:
            place = lanes + low
            return place & (LANES - 1), place >= LANES
        place = lanes - low
        return place & (LANES - 1), place < 0

    def move(chunks, column, sign, rows):
        index, crossed = rotate_index(column, sign, rows)
        zero = jnp.zeros((rows, LANES), jnp.float32)
        turned = [jnp.take_along_axis(chunk, index, axis=1) for chunk in chunks]

        def at(items, place):
            return items[place] if 0 <= place < outer else zero

        moved = [jnp.where(crossed, at(turned, a + sign), turned[a]) for a in range(outer)]
        for bit in range(q_bits):
            chosen = jnp.broadcast_to((column >> (7 + bit)) & 1, (rows, LANES)) == 1
            stride = sign << bit if sign > 0 else -(1 << bit)
            moved = [jnp.where(chosen, at(moved, a + stride), moved[a]) for a in range(outer)]
        return moved

    def halo_copies(s):
        base = pl.multiple_of(s * ext_rows, 8)
        to_right = pltpu.make_async_remote_copy(
            src_ref=ext.at[pl.ds(base + chan_local * outer, halo_rows)],
            dst_ref=ext.at[pl.ds(base, halo_rows)],
            send_sem=halo_send.at[s, 0],
            recv_sem=halo_recv.at[s, 0],
            device_id=(part, right),
            device_id_type=mesh_id,
        )
        to_left = pltpu.make_async_remote_copy(
            src_ref=ext.at[pl.ds(base + halo_rows, halo_rows)],
            dst_ref=ext.at[pl.ds(base + halo_rows + chan_local * outer, halo_rows)],
            send_sem=halo_send.at[s, 1],
            recv_sem=halo_recv.at[s, 1],
            device_id=(part, left),
            device_id_type=mesh_id,
        )
        return to_right, to_left

    def part_copy(s, offset):
        other = lax.rem(part + offset, groups)
        return pltpu.make_async_remote_copy(
            src_ref=up.at[s, other],
            dst_ref=got.at[part * shot_local + s],
            send_sem=part_send.at[s, offset - 1],
            recv_sem=part_recv.at[s, offset - 1],
            device_id=(other, block),
            device_id_type=mesh_id,
        )

    def align(s):
        row = shifts[pl.ds(s, 1), :]
        for top in range(0, chan_local, 8):
            column = to_sublanes(row, 8, top)
            chunks = [traces[s, top : top + 8, a * LANES : (a + 1) * LANES] for a in range(outer)]
            moved = move(chunks, column, 1, 8)
            for a in range(outer):
                start = s * ext_rows + (HALO + top) * outer + a
                ext[pl.ds(start, 8, stride=outer), :] = moved[a]

    def send_halos(s):
        to_right, to_left = halo_copies(s)

        @pl.when(has_right)
        def _():
            to_right.start()

        @pl.when(has_left)
        def _():
            to_left.start()

    small_loads[0].wait()
    trace_loads[0].wait()
    align(0)
    expected = has_left.astype(jnp.int32) + has_right.astype(jnp.int32) + (groups - 1)
    pl.semaphore_wait(barrier, expected)
    send_halos(0)

    def align_step(s, carry):
        align(s)
        send_halos(s)
        return carry

    for load in trace_loads[1:]:
        load.wait()
    lax.fori_loop(1, shot_local, align_step, 0)
    for load in small_loads[1:]:
        load.wait()

    @pl.when(jnp.logical_not(has_left))
    def _():
        for s in range(shot_local):
            ext[s * ext_rows : s * ext_rows + halo_rows, :] = jnp.zeros((halo_rows, LANES), jnp.float32)

    @pl.when(jnp.logical_not(has_right))
    def _():
        for s in range(shot_local):
            ext[(s + 1) * ext_rows - halo_rows : (s + 1) * ext_rows, :] = jnp.zeros(
                (halo_rows, LANES), jnp.float32
            )

    def forward(load, shot_id):
        values = real_dft([load(a) for a in range(outer)])
        for c in range(half):
            re, im = values[c]
            cos, sin = twist[0, c : c + 1, :], twist[1, c : c + 1, :]
            spec[shot_id, c, :, 0:LANES] = re * cos + im * sin
            spec[shot_id, c, :, LANES : 2 * LANES] = im * cos - re * sin
        padded = spec.shape[1]
        if padded > half:
            spec[shot_id, half:padded] = jnp.zeros((padded - half, rec, 2 * LANES), jnp.float32)
        flat = spec[shot_id].reshape(padded * rec, 2 * LANES)
        flat = split_dot(flat, fwd_hi[...], fwd_lo[...])
        spec[shot_id] = flat.reshape(padded, rec, 2 * LANES)

    edge_low = jnp.broadcast_to(has_left, (8, LANES))
    edge_high = jnp.broadcast_to(has_right, (8, LANES))

    def clean_step(s, carry):
        to_right, to_left = halo_copies(s)

        @pl.when(has_left)
        def _():
            to_right.wait_recv()

        @pl.when(has_right)
        def _():
            to_left.wait_recv()

        base = s * ext_rows

        def median_step(tile, carry):
            def rows_at(j):
                return ext[pl.ds(pl.multiple_of(base + j * outer + tile * 8, 8), 8), :]

            rows = {j: rows_at(j) for j in range(chan_local + 2 * HALO)}
            centers = list(range(REACH, chan_local + 2 * HALO - REACH))
            found = median_rows(rows, centers)
            cleaned = {}
            for j in centers:
                value = rows[j] - found[j]
                if j < HALO:
                    value = jnp.where(edge_low, value, 0.0)
                elif j >= HALO + chan_local:
                    value = jnp.where(edge_high, value, 0.0)
                cleaned[j] = value
            centers = list(range(HALO, HALO + chan_local))
            found = median_rows(cleaned, centers)
            for j in centers:
                start = pl.multiple_of((j - HALO) * outer + tile * 8, 8)
                second[pl.ds(start, 8), :] = cleaned[j] - found[j]
            return carry

        lax.fori_loop(0, outer // 8, median_step, 0)

        shot_id = part * shot_local + s
        row = shifts[pl.ds(s, 1), :]
        for g in range(groups):
            column = to_sublanes(row, rec, g * rec)
            low = to_sublanes(lo_ref[...], rec, g * rec)
            high = to_sublanes(hi_ref[...], rec, g * rec)
            inside = jnp.broadcast_to(((low <= shot_id) & (high > shot_id)).astype(jnp.int32), (rec, LANES)) == 1
            chunks = [
                second[pl.ds(g * rec * outer + a, rec, stride=outer), :] for a in range(outer)
            ]
            moved = move(chunks, column, -1, rec)
            for a in range(outer):
                up[s, g, a] = jnp.where(inside, moved[a], 0.0)
        for offset in range(1, groups):
            part_copy(s, offset).start()
        forward(lambda a: up[s, part, a], shot_id)

        @pl.when(s > 0)
        def _():
            arrive(s - 1)

        return carry

    def arrive(s):
        for offset in range(1, groups):
            part_copy(s, offset).wait_recv()
            source = lax.rem(part + groups - offset, groups)
            shot_id = source * shot_local + s
            forward(lambda a: got[shot_id, a], shot_id)

    lax.fori_loop(0, shot_local, clean_step, 0)
    arrive(shot_local - 1)

    band = jnp.broadcast_to(to_sublanes(band_ref[...], rec, part * rec), (rec, LANES))
    lane_ids = lax.broadcasted_iota(jnp.int32, (rec, LANES), 1)

    def dip_step(c, carry):
        frequency = lane_ids * outer + c
        freq_abs = jnp.minimum(frequency, length - frequency)
        values = [
            (spec[s, c, :, 0:LANES], spec[s, c, :, LANES : 2 * LANES]) for s in range(shots)
        ]
        waves = complex_dft(values, -1)
        kept = []
        for k in range(shots):
            keep = min(k, shots - k) * band <= freq_abs
            kept.append((jnp.where(keep, waves[k][0], 0.0), jnp.where(keep, waves[k][1], 0.0)))
        values = complex_dft(kept, 1)
        for s in range(shots):
            spec[s, c, :, 0:LANES] = values[s][0]
            spec[s, c, :, LANES : 2 * LANES] = values[s][1]
        return carry

    lax.fori_loop(0, half, dip_step, 0)

    padded = spec.shape[1]
    batch = shots // 2
    for first in range(0, shots, batch):
        flat = spec[first : first + batch].reshape(batch * padded * rec, 2 * LANES)
        flat = split_dot(flat, inv_hi[...], inv_lo[...])
        spec[first : first + batch] = flat.reshape(batch, padded, rec, 2 * LANES)

    def back_step(s, carry):
        values = []
        for c in range(half):
            re, im = spec[s, c, :, 0:LANES], spec[s, c, :, LANES : 2 * LANES]
            cos, sin = twist[0, c : c + 1, :], twist[1, c : c + 1, :]
            values.append((re * cos - im * sin, im * cos + re * sin))
        for a, value in enumerate(real_inverse(values, outer)):
            out[s, :, a * LANES : (a + 1) * LANES] = value
        return carry

    lax.fori_loop(0, shots, back_step, 0)

    def drain_step(s, carry):
        to_right, to_left = halo_copies(s)

        @pl.when(has_right)
        def _():
            to_right.wait_send()

        @pl.when(has_left)
        def _():
            to_left.wait_send()

        for offset in range(1, groups):
            part_copy(s, offset).wait_send()
        return carry

    lax.fori_loop(0, shot_local, drain_step, 0)


def halves(table):
    high = table.astype(jnp.bfloat16)
    return high, (table - high.astype(np.float64)).astype(jnp.bfloat16)


def tables(shots, length):
    outer = length // LANES
    ids = np.arange(LANES)
    angles = 2.0 * np.pi * (np.outer(ids, ids) % LANES) / LANES
    cos, sin = np.cos(angles), np.sin(angles)
    forward = np.block([[cos, -sin], [sin, cos]])
    inverse = np.block([[cos, sin], [-sin, cos]]) / (shots * length)
    product = np.outer(np.arange(outer // 2 + 1), ids) % length
    angles = 2.0 * np.pi * product / length
    twist = np.stack([np.cos(angles), np.sin(angles)]).astype(np.float32)
    return halves(forward) + halves(inverse) + (twist,)


def local(groups, blocks, traces, shifts, aperture_lo, aperture_hi, dip_band):
    shot_local, chan_local, length = traces.shape
    outer = length // LANES
    rec = chan_local // groups
    shots = groups * shot_local
    padded = outer // 2 + 2
    constants = [jnp.asarray(table) for table in tables(shots, length)]
    operands = [
        traces, shifts, aperture_lo[None, :], aperture_hi[None, :], dip_band[None, :], *constants
    ]
    others = max(groups - 1, 1)
    return pl.pallas_call(
        functools.partial(kernel, groups, blocks),
        out_shape=jax.ShapeDtypeStruct((shots, rec, length), jnp.float32),
        in_specs=[pl.BlockSpec(memory_space=pltpu.HBM)] * len(operands),
        out_specs=pl.BlockSpec(memory_space=pltpu.VMEM),
        scratch_shapes=[pltpu.VMEM(item.shape, item.dtype) for item in operands] + [
            pltpu.VMEM((shot_local * (chan_local + 2 * HALO) * outer, LANES), jnp.float32),
            pltpu.VMEM((chan_local * outer, LANES), jnp.float32),
            pltpu.VMEM((shot_local, groups, outer, rec, LANES), jnp.float32),
            pltpu.VMEM((shots, outer, rec, LANES), jnp.float32),
            pltpu.VMEM((shots, padded, rec, 2 * LANES), jnp.float32),
            pltpu.SemaphoreType.DMA((shot_local, 2)),
            pltpu.SemaphoreType.DMA((shot_local, 2)),
            pltpu.SemaphoreType.DMA((shot_local, others)),
            pltpu.SemaphoreType.DMA((shot_local, others)),
            pltpu.SemaphoreType.DMA((shot_local,)),
            pltpu.SemaphoreType.DMA((len(operands) - 1,)),
        ],
        compiler_params=pltpu.CompilerParams(
            collective_id=0, has_side_effects=True, vmem_limit_bytes=48 * 1024 * 1024
        ),
    )(*operands)


def solution(mesh):
    return jax.shard_map(
        functools.partial(local, mesh.shape["shot"], mesh.shape["chan"]),
        mesh=mesh,
        in_specs=(P("shot", "chan", None), P("shot", "chan"), P("chan"), P("chan"), P("chan")),
        out_specs=P(None, ("chan", "shot"), None),
        check_vma=False,
    )
```

```python
import functools
import math

import jax
import jax.numpy as jnp
import numpy as np
from jax import lax
from jax.experimental import pallas as pl
from jax.experimental.pallas import tpu as pltpu
from jax.sharding import PartitionSpec as P

LANES = 128
REACH = 5
HALO = 2 * REACH


def sort_two(a, b):
    return jnp.minimum(a, b), jnp.maximum(a, b)


def median_rows(rows, centers):
    pairs = {}
    fours = {}
    results = {}

    def pair(at):
        if at not in pairs:
            pairs[at] = sort_two(rows[at], rows[at + 1])
        return pairs[at]

    def four(at):
        if at not in fours:
            a, b = pair(at)
            c, d = pair(at + 2)
            low, mid_a = sort_two(a, c)
            mid_b, high = sort_two(b, d)
            mid_a, mid_b = sort_two(mid_a, mid_b)
            fours[at] = (low, mid_a, mid_b, high)
        return fours[at]

    def middle_two(core, extra):
        a, b, c, d = core
        p, q = extra
        low = jnp.minimum(c, jnp.minimum(jnp.maximum(b, p), jnp.maximum(a, q)))
        high = jnp.maximum(b, jnp.maximum(jnp.minimum(d, p), jnp.minimum(c, q)))
        return low, high

    def clamp(value, ends):
        return jnp.maximum(ends[0], jnp.minimum(value, ends[1]))

    last = centers[-1]
    for c in centers[::4]:
        x, y = four(c - 2), four(c + 2)
        low = [jnp.minimum(x[i], y[3 - i]) for i in range(4)]
        high = [jnp.maximum(x[i], y[3 - i]) for i in range(4)]
        core = sort_two(jnp.maximum(low[0], low[2]), jnp.maximum(low[1], low[3])) + sort_two(
            jnp.minimum(high[0], high[2]), jnp.minimum(high[1], high[3])
        )
        ends = middle_two(core, pair(c - 4))
        results[c] = clamp(rows[c - 5], ends)
        results[c + 1] = clamp(rows[c + 6], ends)
        if c + 2 <= last:
            ends = middle_two(core, pair(c + 6))
            results[c + 2] = clamp(rows[c - 3], ends)
            results[c + 3] = clamp(rows[c + 8], ends)
    return results


def turn(value, angle_index, size, sign):
    re, im = value
    angle_index = angle_index % size
    if angle_index == 0:
        return value
    if 4 * angle_index == size:
        return (-im, re) if sign > 0 else (im, -re)
    if 2 * angle_index == size:
        return (-re, -im)
    angle = 2.0 * math.pi * angle_index / size
    cos, sin = math.cos(angle), sign * math.sin(angle)
    if 8 * angle_index == size:
        return ((re - im) * cos, (re + im) * cos) if sign > 0 else ((re + im) * cos, (im - re) * cos)
    return (re * cos - im * sin, re * sin + im * cos)


def add(a, b):
    return (a[0] + b[0], a[1] + b[1])


def sub(a, b):
    return (a[0] - b[0], a[1] - b[1])


def conj(a):
    return (a[0], -a[1])


def complex_dft(values, sign):
    size = len(values)
    if size == 1:
        return values
    even = complex_dft(values[0::2], sign)
    odd = complex_dft(values[1::2], sign)
    odd = [turn(odd[k], k, size, sign) for k in range(size // 2)]
    return [add(even[k], odd[k]) for k in range(size // 2)] + [
        sub(even[k], odd[k]) for k in range(size // 2)
    ]


def real_dft(values):
    size = len(values)
    if size == 2:
        zero = jnp.zeros_like(values[0])
        return [(values[0] + values[1], zero), (values[0] - values[1], zero)]
    even, odd = real_dft(values[0::2]), real_dft(values[1::2])
    half = size // 2
    zero = jnp.zeros_like(values[0])
    result = [None] * (half + 1)
    result[0] = (even[0][0] + odd[0][0], zero)
    result[half] = (even[0][0] - odd[0][0], zero)
    for k in range(1, half // 2 + 1):
        if 2 * k == half:
            result[k] = (even[k][0], -odd[k][0])
        else:
            moved = turn(odd[k], k, size, -1)
            result[k] = add(even[k], moved)
            result[half - k] = conj(sub(even[k], moved))
    return result


def real_inverse(values, size):
    half = size // 2
    if size == 2:
        a, b = values[0][0], values[1][0]
        return [a + b, a - b]
    even, odd = [], []
    for k in range(half // 2 + 1):
        if k == 0:
            even.append((values[0][0] + values[half][0], None))
            odd.append((values[0][0] - values[half][0], None))
        elif 2 * k == half:
            even.append((2.0 * values[k][0], None))
            odd.append((-2.0 * values[k][1], None))
        else:
            other = conj(values[half - k])
            even.append(add(values[k], other))
            odd.append(turn(sub(values[k], other), k, size, 1))
    first, second = real_inverse(even, half), real_inverse(odd, half)
    return [item for both in zip(first, second) for item in both]


def split_dot(x, high_table, low_table):
    high = x.astype(jnp.bfloat16)
    low = (x - high.astype(jnp.float32)).astype(jnp.bfloat16)

    def dot(a, b):
        return jnp.dot(a, b, preferred_element_type=jnp.float32)

    return dot(high, high_table) + (dot(low, high_table) + dot(high, low_table))


def to_sublanes(row, count, start):
    size = row.shape[1]
    row_ids = lax.broadcasted_iota(jnp.int32, (count, size), 0)
    col_ids = lax.broadcasted_iota(jnp.int32, (count, size), 1)
    spread = jnp.broadcast_to(row.astype(jnp.float32), (count, size))
    picked = jnp.where(col_ids == row_ids + start, spread, 0.0)
    return jnp.sum(picked, axis=1, keepdims=True).astype(jnp.int32)


def kernel(
    groups, blocks,
    traces_hbm, *rest,
):
    small_hbm, out_hbm, scratch = rest[:6], rest[6], rest[7:]
    traces, small, scratch = scratch[0], scratch[1:7], scratch[7:]
    shifts, lo_ref, hi_ref, band_ref, table, twist = small
    ext, second, up, got, spec, out, table_hi, table_lo = scratch[:8]
    halo_send, halo_recv, part_send, part_recv, load_sem, small_sem, out_sem = scratch[8:]
    shot_local, chan_local, length = traces.shape
    outer = length // LANES
    half = outer // 2 + 1
    rec = chan_local // groups
    shots = groups * shot_local
    tiles = outer // 8
    back = outer // 4
    span = outer + back
    unit_rows = (chan_local + 2 * HALO) * 8
    halo_rows = HALO * 8
    part = lax.axis_index("shot")
    block = lax.axis_index("chan")
    mesh_id = pl.DeviceIdType.MESH
    has_left = block > 0
    has_right = block < blocks - 1
    left = jnp.maximum(block - 1, 0)
    right = jnp.minimum(block + 1, blocks - 1)
    q_bits = max((length // 4 // LANES - 1).bit_length(), 0)

    small_loads = [
        pltpu.make_async_copy(small_hbm[i], small[i], small_sem.at[i]) for i in range(len(small))
    ]
    trace_loads = [
        pltpu.make_async_copy(traces_hbm.at[s], traces.at[s], load_sem.at[s]) for s in range(shot_local)
    ]
    small_loads[0].start()
    for load in trace_loads + small_loads[1:]:
        load.start()

    barrier = pltpu.get_barrier_semaphore()

    @pl.when(has_left)
    def _():
        pl.semaphore_signal(barrier, inc=1, device_id=(part, left), device_id_type=mesh_id)

    @pl.when(has_right)
    def _():
        pl.semaphore_signal(barrier, inc=1, device_id=(part, right), device_id_type=mesh_id)

    for offset in range(1, groups):
        pl.semaphore_signal(
            barrier, inc=1, device_id=(lax.rem(part + offset, groups), block), device_id_type=mesh_id
        )

    def rotate_index(column, sign, rows):
        lanes = lax.broadcasted_iota(jnp.int32, (rows, LANES), 1)
        low = jnp.broadcast_to(column & (LANES - 1), (rows, LANES))
        if sign > 0:
            place = lanes + low
            return place & (LANES - 1), place >= LANES
        place = lanes - low
        return place & (LANES - 1), place < 0

    def whole_chunks(column, rows):
        return [
            jnp.broadcast_to((column >> (7 + bit)) & 1, (rows, LANES)) == 1 for bit in range(q_bits)
        ]

    def move_earlier(chunks, column, rows):
        index, crossed = rotate_index(column, 1, rows)
        zero = jnp.zeros((rows, LANES), jnp.float32)
        turned = [jnp.take_along_axis(chunk, index, axis=1) for chunk in chunks]

        def at(items, place):
            return items[place] if place < outer else zero

        moved = [jnp.where(crossed, at(turned, a + 1), turned[a]) for a in range(outer)]
        for bit, chosen in enumerate(whole_chunks(column, rows)):
            moved = [jnp.where(chosen, at(moved, a + (1 << bit)), moved[a]) for a in range(outer)]
        return moved

    def move_later(chunks, chosen, index, crossed):
        moved = dict(enumerate(chunks))
        first = back + 8 - len(chunks)
        for bit in reversed(range(q_bits)):
            first += 1 << bit
            moved = {
                a: jnp.where(chosen[bit], moved[a - (1 << bit)], moved[a])
                for a in range(first, back + 8)
            }
        turned = {a: jnp.take_along_axis(moved[a], index, axis=1) for a in range(back - 1, back + 8)}
        return [jnp.where(crossed, turned[a - 1], turned[a]) for a in range(back, back + 8)]

    def halo_copies(unit):
        base = pl.multiple_of(unit * unit_rows, 8)
        to_right = pltpu.make_async_remote_copy(
            src_ref=ext.at[pl.ds(base + chan_local * 8, halo_rows)],
            dst_ref=ext.at[pl.ds(base, halo_rows)],
            send_sem=halo_send.at[unit, 0],
            recv_sem=halo_recv.at[unit, 0],
            device_id=(part, right),
            device_id_type=mesh_id,
        )
        to_left = pltpu.make_async_remote_copy(
            src_ref=ext.at[pl.ds(base + halo_rows, halo_rows)],
            dst_ref=ext.at[pl.ds(base + halo_rows + chan_local * 8, halo_rows)],
            send_sem=halo_send.at[unit, 1],
            recv_sem=halo_recv.at[unit, 1],
            device_id=(part, left),
            device_id_type=mesh_id,
        )
        return to_right, to_left

    def part_copy(s, tile, offset):
        other = lax.rem(part + offset, groups)
        rows = pl.ds(pl.multiple_of(tile * 8, 8), 8)
        return pltpu.make_async_remote_copy(
            src_ref=up.at[s, other, rows],
            dst_ref=got.at[part * shot_local + s, rows],
            send_sem=part_send.at[s * tiles + tile, offset - 1],
            recv_sem=part_recv.at[s * tiles + tile, offset - 1],
            device_id=(other, block),
            device_id_type=mesh_id,
        )

    def align(s):
        row = shifts[pl.ds(s, 1), :]
        for top in range(0, chan_local, 8):
            column = to_sublanes(row, 8, top)
            chunks = [traces[s, top : top + 8, a * LANES : (a + 1) * LANES] for a in range(outer)]
            moved = move_earlier(chunks, column, 8)
            for a in range(outer):
                start = (s * tiles + a // 8) * unit_rows + (HALO + top) * 8 + a % 8
                ext[pl.ds(start, 8, stride=8), :] = moved[a]

    def send_halos(s):
        for tile in range(tiles):
            to_right, to_left = halo_copies(s * tiles + tile)
            pl.when(has_right)(to_right.start)
            pl.when(has_left)(to_left.start)

    small_loads[0].wait()
    trace_loads[0].wait()
    align(0)
    expected = has_left.astype(jnp.int32) + has_right.astype(jnp.int32) + (groups - 1)
    pl.semaphore_wait(barrier, expected)
    send_halos(0)

    def align_step(s, carry):
        align(s)
        send_halos(s)
        return carry

    for load in trace_loads[1:]:
        load.wait()
    lax.fori_loop(1, shot_local, align_step, 0)
    for load in small_loads[1:]:
        load.wait()
    table_hi[...] = table[...].astype(jnp.bfloat16)
    table_lo[...] = (table[...] - table_hi[...].astype(jnp.float32)).astype(jnp.bfloat16)

    def clear(first):
        def clear_step(unit, carry):
            rows = pl.ds(pl.multiple_of(unit * unit_rows + first, 8), halo_rows)
            ext[rows, :] = jnp.zeros((halo_rows, LANES), jnp.float32)
            return carry

        lax.fori_loop(0, shot_local * tiles, clear_step, 0)

    pl.when(jnp.logical_not(has_left))(lambda: clear(0))
    pl.when(jnp.logical_not(has_right))(lambda: clear(halo_rows + chan_local * 8))
    for c in range(chan_local):
        second[c * span : c * span + back, :] = jnp.zeros((back, LANES), jnp.float32)

    def forward(load, shot_id):
        values = real_dft([load(a) for a in range(outer)])
        for c in range(half):
            re, im = values[c]
            cos, sin = twist[0, c : c + 1, :], twist[1, c : c + 1, :]
            spec[shot_id, c, :, 0:LANES] = re * cos + im * sin
            spec[shot_id, c, :, LANES : 2 * LANES] = im * cos - re * sin
        padded = spec.shape[1]
        if padded > half:
            spec[shot_id, half:padded] = jnp.zeros((padded - half, rec, 2 * LANES), jnp.float32)
        flat = spec[shot_id].reshape(padded * rec, 2 * LANES)
        flat = split_dot(flat, table_hi[...], table_lo[...])
        spec[shot_id] = flat.reshape(padded, rec, 2 * LANES)

    edge_low = jnp.broadcast_to(has_left, (8, LANES))
    edge_high = jnp.broadcast_to(has_right, (8, LANES))

    def clean_step(s, carry):
        shot_id = part * shot_local + s
        row = shifts[pl.ds(s, 1), :]
        moves = []
        for g in range(groups):
            column = to_sublanes(row, rec, g * rec)
            low = to_sublanes(lo_ref[...], rec, g * rec)
            high = to_sublanes(hi_ref[...], rec, g * rec)
            inside = ((low <= shot_id) & (high > shot_id)).astype(jnp.int32)
            inside = jnp.broadcast_to(inside, (rec, LANES)) == 1
            moves.append((whole_chunks(column, rec),) + rotate_index(column, -1, rec) + (inside,))

        def unit_step(tile, carry):
            unit = s * tiles + tile
            to_right, to_left = halo_copies(unit)
            pl.when(has_left)(to_right.wait_recv)
            pl.when(has_right)(to_left.wait_recv)
            base = unit * unit_rows

            def rows_at(j):
                return ext[pl.ds(pl.multiple_of(base + j * 8, 8), 8), :]

            rows = {j: rows_at(j) for j in range(chan_local + 2 * HALO)}
            centers = list(range(REACH, chan_local + 2 * HALO - REACH))
            found = median_rows(rows, centers)
            cleaned = {}
            for j in centers:
                value = rows[j] - found[j]
                if j < HALO:
                    value = jnp.where(edge_low, value, 0.0)
                elif j >= HALO + chan_local:
                    value = jnp.where(edge_high, value, 0.0)
                cleaned[j] = value
            centers = list(range(HALO, HALO + chan_local))
            found = median_rows(cleaned, centers)
            for j in centers:
                start = pl.multiple_of((j - HALO) * span + back + tile * 8, 8)
                second[pl.ds(start, 8), :] = cleaned[j] - found[j]

            for g in range(groups):
                chosen, index, crossed, inside = moves[g]
                chunks = [
                    second[pl.ds(g * rec * span + tile * 8 + a, rec, stride=span), :]
                    for a in range(back + 8)
                ]
                for a, value in enumerate(move_later(chunks, chosen, index, crossed)):
                    up[s, g, tile * 8 + a] = jnp.where(inside, value, 0.0)
            for offset in range(1, groups):
                part_copy(s, tile, offset).start()
            return carry

        lax.fori_loop(0, tiles, unit_step, 0)
        forward(lambda a: up[s, part, a], shot_id)

        @pl.when(s > 0)
        def _():
            arrive(s - 1)

        return carry

    def arrive(s):
        for offset in range(1, groups):
            for tile in range(tiles):
                part_copy(s, tile, offset).wait_recv()
            source = lax.rem(part + groups - offset, groups)
            shot_id = source * shot_local + s
            forward(lambda a: got[shot_id, a], shot_id)

    lax.fori_loop(0, shot_local, clean_step, 0)
    arrive(shot_local - 1)

    band = jnp.broadcast_to(to_sublanes(band_ref[...], rec, part * rec), (rec, LANES))
    lane_ids = lax.broadcasted_iota(jnp.int32, (rec, LANES), 1)

    def dip_step(c, carry):
        frequency = lane_ids * outer + c
        freq_abs = jnp.minimum(frequency, length - frequency)
        values = [
            (spec[s, c, :, 0:LANES], spec[s, c, :, LANES : 2 * LANES]) for s in range(shots)
        ]
        waves = complex_dft(values, -1)
        kept = []
        for k in range(shots):
            keep = min(k, shots - k) * band <= freq_abs
            kept.append((jnp.where(keep, waves[k][0], 0.0), jnp.where(keep, waves[k][1], 0.0)))
        values = complex_dft(kept, 1)
        for s in range(shots):
            spec[s, c, :, 0:LANES] = values[s][0]
            spec[s, c, :, LANES : 2 * LANES] = -values[s][1]
        return carry

    lax.fori_loop(0, half, dip_step, 0)

    padded = spec.shape[1]
    batch = shots // 2
    for first in range(0, shots, batch):
        flat = spec[first : first + batch].reshape(batch * padded * rec, 2 * LANES)
        flat = split_dot(flat, table_hi[...], table_lo[...])
        spec[first : first + batch] = flat.reshape(batch, padded, rec, 2 * LANES)

    def out_copy(s):
        return pltpu.make_async_copy(out.at[s], out_hbm.at[s], out_sem.at[s])

    def back_step(s, carry):
        values = []
        for c in range(half):
            re, minus = spec[s, c, :, 0:LANES], spec[s, c, :, LANES : 2 * LANES]
            cos, sin = twist[2, c : c + 1, :], twist[3, c : c + 1, :]
            values.append((re * cos + minus * sin, re * sin - minus * cos))
        for a, value in enumerate(real_inverse(values, outer)):
            out[s, :, a * LANES : (a + 1) * LANES] = value
        out_copy(s).start()
        return carry

    lax.fori_loop(0, shots, back_step, 0)

    def drain_step(unit, carry):
        to_right, to_left = halo_copies(unit)
        pl.when(has_right)(to_right.wait_send)
        pl.when(has_left)(to_left.wait_send)
        for offset in range(1, groups):
            part_copy(unit // tiles, unit % tiles, offset).wait_send()
        return carry

    lax.fori_loop(0, shot_local * tiles, drain_step, 0)
    for s in range(shots):
        out_copy(s).wait()


def tables(shots, length):
    outer = length // LANES
    ids = np.arange(LANES)
    angles = 2.0 * np.pi * (np.outer(ids, ids) % LANES) / LANES
    cos, sin = np.cos(angles), np.sin(angles)
    table = np.block([[cos, -sin], [sin, cos]]).astype(np.float32)
    product = np.outer(np.arange(outer // 2 + 1), ids) % length
    angles = 2.0 * np.pi * product / length
    twist = np.stack([np.cos(angles), np.sin(angles)])
    return table, np.concatenate([twist / (shots * length), twist]).astype(np.float32)


def local(groups, blocks, traces, shifts, aperture_lo, aperture_hi, dip_band):
    shot_local, chan_local, length = traces.shape
    outer = length // LANES
    rec = chan_local // groups
    shots = groups * shot_local
    padded = outer // 2 + 2
    constants = [jnp.asarray(item) for item in tables(shots, length)]
    operands = [
        traces, shifts, aperture_lo[None, :], aperture_hi[None, :], dip_band[None, :], *constants
    ]
    others = max(groups - 1, 1)
    units = shot_local * (outer // 8)
    return pl.pallas_call(
        functools.partial(kernel, groups, blocks),
        out_shape=jax.ShapeDtypeStruct((shots, rec, length), jnp.float32),
        in_specs=[pl.BlockSpec(memory_space=pltpu.HBM)] * len(operands),
        out_specs=pl.BlockSpec(memory_space=pltpu.HBM),
        scratch_shapes=[pltpu.VMEM(item.shape, item.dtype) for item in operands] + [
            pltpu.VMEM((shot_local * (chan_local + 2 * HALO) * outer, LANES), jnp.float32),
            pltpu.VMEM((chan_local * (outer + outer // 4), LANES), jnp.float32),
            pltpu.VMEM((shot_local, groups, outer, rec, LANES), jnp.float32),
            pltpu.VMEM((shots, outer, rec, LANES), jnp.float32),
            pltpu.VMEM((shots, padded, rec, 2 * LANES), jnp.float32),
            pltpu.VMEM((shots, rec, length), jnp.float32),
            pltpu.VMEM((2 * LANES, 2 * LANES), jnp.bfloat16),
            pltpu.VMEM((2 * LANES, 2 * LANES), jnp.bfloat16),
            pltpu.SemaphoreType.DMA((units, 2)),
            pltpu.SemaphoreType.DMA((units, 2)),
            pltpu.SemaphoreType.DMA((units, others)),
            pltpu.SemaphoreType.DMA((units, others)),
            pltpu.SemaphoreType.DMA((shot_local,)),
            pltpu.SemaphoreType.DMA((len(operands) - 1,)),
            pltpu.SemaphoreType.DMA((shots,)),
        ],
        compiler_params=pltpu.CompilerParams(
            collective_id=0, has_side_effects=True, vmem_limit_bytes=60 * 1024 * 1024
        ),
    )(*operands)


def solution(mesh):
    return jax.shard_map(
        functools.partial(local, mesh.shape["shot"], mesh.shape["chan"]),
        mesh=mesh,
        in_specs=(P("shot", "chan", None), P("shot", "chan"), P("chan"), P("chan"), P("chan")),
        out_specs=P(None, ("chan", "shot"), None),
        check_vma=False,
    )
```

```python
import functools
import math

import jax
import jax.numpy as jnp
import numpy as np
from jax import lax
from jax.experimental import pallas as pl
from jax.experimental.pallas import tpu as pltpu
from jax.sharding import PartitionSpec as P

LANES = 128
REACH = 5
HALO = 2 * REACH


def sort_two(a, b):
    return jnp.minimum(a, b), jnp.maximum(a, b)


def median_rows(rows, centers):
    pairs = {}
    fours = {}
    results = {}

    def pair(at):
        if at not in pairs:
            pairs[at] = sort_two(rows[at], rows[at + 1])
        return pairs[at]

    def four(at):
        if at not in fours:
            a, b = pair(at)
            c, d = pair(at + 2)
            low, mid_a = sort_two(a, c)
            mid_b, high = sort_two(b, d)
            mid_a, mid_b = sort_two(mid_a, mid_b)
            fours[at] = (low, mid_a, mid_b, high)
        return fours[at]

    def middle_two(core, extra):
        a, b, c, d = core
        p, q = extra
        low = jnp.minimum(c, jnp.minimum(jnp.maximum(b, p), jnp.maximum(a, q)))
        high = jnp.maximum(b, jnp.maximum(jnp.minimum(d, p), jnp.minimum(c, q)))
        return low, high

    def clamp(value, ends):
        return jnp.maximum(ends[0], jnp.minimum(value, ends[1]))

    last = centers[-1]
    for c in centers[::4]:
        x, y = four(c - 2), four(c + 2)
        low = [jnp.minimum(x[i], y[3 - i]) for i in range(4)]
        high = [jnp.maximum(x[i], y[3 - i]) for i in range(4)]
        core = sort_two(jnp.maximum(low[0], low[2]), jnp.maximum(low[1], low[3])) + sort_two(
            jnp.minimum(high[0], high[2]), jnp.minimum(high[1], high[3])
        )
        ends = middle_two(core, pair(c - 4))
        results[c] = clamp(rows[c - 5], ends)
        results[c + 1] = clamp(rows[c + 6], ends)
        if c + 2 <= last:
            ends = middle_two(core, pair(c + 6))
            results[c + 2] = clamp(rows[c - 3], ends)
            results[c + 3] = clamp(rows[c + 8], ends)
    return results


def turn(value, angle_index, size, sign):
    re, im = value
    angle_index = angle_index % size
    if angle_index == 0:
        return value
    if 4 * angle_index == size:
        return (-im, re) if sign > 0 else (im, -re)
    if 2 * angle_index == size:
        return (-re, -im)
    angle = 2.0 * math.pi * angle_index / size
    cos, sin = math.cos(angle), sign * math.sin(angle)
    if 8 * angle_index == size:
        return ((re - im) * cos, (re + im) * cos) if sign > 0 else ((re + im) * cos, (im - re) * cos)
    return (re * cos - im * sin, re * sin + im * cos)


def add(a, b):
    return (a[0] + b[0], a[1] + b[1])


def sub(a, b):
    return (a[0] - b[0], a[1] - b[1])


def conj(a):
    return (a[0], -a[1])


def complex_dft(values, sign):
    size = len(values)
    if size == 1:
        return values
    even = complex_dft(values[0::2], sign)
    odd = complex_dft(values[1::2], sign)
    odd = [turn(odd[k], k, size, sign) for k in range(size // 2)]
    return [add(even[k], odd[k]) for k in range(size // 2)] + [
        sub(even[k], odd[k]) for k in range(size // 2)
    ]


def real_dft(values):
    size = len(values)
    if size == 2:
        zero = jnp.zeros_like(values[0])
        return [(values[0] + values[1], zero), (values[0] - values[1], zero)]
    even, odd = real_dft(values[0::2]), real_dft(values[1::2])
    half = size // 2
    zero = jnp.zeros_like(values[0])
    result = [None] * (half + 1)
    result[0] = (even[0][0] + odd[0][0], zero)
    result[half] = (even[0][0] - odd[0][0], zero)
    for k in range(1, half // 2 + 1):
        if 2 * k == half:
            result[k] = (even[k][0], -odd[k][0])
        else:
            moved = turn(odd[k], k, size, -1)
            result[k] = add(even[k], moved)
            result[half - k] = conj(sub(even[k], moved))
    return result


def real_inverse(values, size):
    half = size // 2
    if size == 2:
        a, b = values[0][0], values[1][0]
        return [a + b, a - b]
    even, odd = [], []
    for k in range(half // 2 + 1):
        if k == 0:
            even.append((values[0][0] + values[half][0], None))
            odd.append((values[0][0] - values[half][0], None))
        elif 2 * k == half:
            even.append((2.0 * values[k][0], None))
            odd.append((-2.0 * values[k][1], None))
        else:
            other = conj(values[half - k])
            even.append(add(values[k], other))
            odd.append(turn(sub(values[k], other), k, size, 1))
    first, second = real_inverse(even, half), real_inverse(odd, half)
    return [item for both in zip(first, second) for item in both]


def split_dot(x, high_table, low_table):
    high = x.astype(jnp.bfloat16)
    low = (x - high.astype(jnp.float32)).astype(jnp.bfloat16)

    def dot(a, b):
        return jnp.dot(a, b, preferred_element_type=jnp.float32)

    return dot(high, high_table) + (dot(low, high_table) + dot(high, low_table))


def to_sublanes(row, count, start):
    size = row.shape[1]
    row_ids = lax.broadcasted_iota(jnp.int32, (count, size), 0)
    col_ids = lax.broadcasted_iota(jnp.int32, (count, size), 1)
    spread = jnp.broadcast_to(row.astype(jnp.float32), (count, size))
    picked = jnp.where(col_ids == row_ids + start, spread, 0.0)
    return jnp.sum(picked, axis=1, keepdims=True).astype(jnp.int32)


def kernel(
    groups, blocks,
    traces_hbm, *rest,
):
    small_hbm, out_hbm, scratch = rest[:6], rest[6], rest[7:]
    traces, small, scratch = scratch[0], scratch[1:7], scratch[7:]
    shifts, lo_ref, hi_ref, band_ref, table, twist = small
    ext, second, up, got, spec, out, table_hi, table_lo = scratch[:8]
    halo_send, halo_recv, part_send, part_recv, load_sem, small_sem, out_sem = scratch[8:]
    shot_local, chan_local, length = traces.shape
    outer = length // LANES
    half = outer // 2 + 1
    rec = chan_local // groups
    shots = groups * shot_local
    tiles = outer // 8
    back = outer // 4
    span = outer + back
    unit_rows = (chan_local + 2 * HALO) * 8
    halo_rows = HALO * 8
    part = lax.axis_index("shot")
    block = lax.axis_index("chan")
    mesh_id = pl.DeviceIdType.MESH
    has_left = block > 0
    has_right = block < blocks - 1
    left = jnp.maximum(block - 1, 0)
    right = jnp.minimum(block + 1, blocks - 1)
    q_bits = max((length // 4 // LANES - 1).bit_length(), 0)

    small_loads = [
        pltpu.make_async_copy(small_hbm[i], small[i], small_sem.at[i]) for i in range(len(small))
    ]
    trace_loads = [
        pltpu.make_async_copy(traces_hbm.at[s], traces.at[s], load_sem.at[s]) for s in range(shot_local)
    ]
    small_loads[0].start()
    for load in trace_loads + small_loads[1:]:
        load.start()

    barrier = pltpu.get_barrier_semaphore()

    @pl.when(has_left)
    def _():
        pl.semaphore_signal(barrier, inc=1, device_id=(part, left), device_id_type=mesh_id)

    @pl.when(has_right)
    def _():
        pl.semaphore_signal(barrier, inc=1, device_id=(part, right), device_id_type=mesh_id)

    for offset in range(1, groups):
        pl.semaphore_signal(
            barrier, inc=1, device_id=(lax.rem(part + offset, groups), block), device_id_type=mesh_id
        )

    def rotate_index(column, sign, rows):
        lanes = lax.broadcasted_iota(jnp.int32, (rows, LANES), 1)
        low = jnp.broadcast_to(column & (LANES - 1), (rows, LANES))
        if sign > 0:
            place = lanes + low
            return place & (LANES - 1), place >= LANES
        place = lanes - low
        return place & (LANES - 1), place < 0

    def whole_chunks(column, rows):
        return [
            jnp.broadcast_to((column >> (7 + bit)) & 1, (rows, LANES)) == 1 for bit in range(q_bits)
        ]

    def move_earlier(chunks, column, rows):
        index, crossed = rotate_index(column, 1, rows)
        zero = jnp.zeros((rows, LANES), jnp.float32)
        turned = [jnp.take_along_axis(chunk, index, axis=1) for chunk in chunks]

        def at(items, place):
            return items[place] if place < outer else zero

        moved = [jnp.where(crossed, at(turned, a + 1), turned[a]) for a in range(outer)]
        for bit, chosen in enumerate(whole_chunks(column, rows)):
            moved = [jnp.where(chosen, at(moved, a + (1 << bit)), moved[a]) for a in range(outer)]
        return moved

    def move_later(chunks, chosen, index, crossed):
        moved = dict(enumerate(chunks))
        first = back + 8 - len(chunks)
        for bit in reversed(range(q_bits)):
            first += 1 << bit
            moved = {
                a: jnp.where(chosen[bit], moved[a - (1 << bit)], moved[a])
                for a in range(first, back + 8)
            }
        turned = {a: jnp.take_along_axis(moved[a], index, axis=1) for a in range(back - 1, back + 8)}
        return [jnp.where(crossed, turned[a - 1], turned[a]) for a in range(back, back + 8)]

    def halo_copies(unit):
        base = pl.multiple_of(unit * unit_rows, 8)
        to_right = pltpu.make_async_remote_copy(
            src_ref=ext.at[pl.ds(base + chan_local * 8, halo_rows)],
            dst_ref=ext.at[pl.ds(base, halo_rows)],
            send_sem=halo_send.at[unit, 0],
            recv_sem=halo_recv.at[unit, 0],
            device_id=(part, right),
            device_id_type=mesh_id,
        )
        to_left = pltpu.make_async_remote_copy(
            src_ref=ext.at[pl.ds(base + halo_rows, halo_rows)],
            dst_ref=ext.at[pl.ds(base + halo_rows + chan_local * 8, halo_rows)],
            send_sem=halo_send.at[unit, 1],
            recv_sem=halo_recv.at[unit, 1],
            device_id=(part, left),
            device_id_type=mesh_id,
        )
        return to_right, to_left

    def part_copy(s, tile, offset):
        other = lax.rem(part + offset, groups)
        rows = pl.ds(pl.multiple_of(tile * 8, 8), 8)
        return pltpu.make_async_remote_copy(
            src_ref=up.at[s, other, rows],
            dst_ref=got.at[part * shot_local + s, rows],
            send_sem=part_send.at[s * tiles + tile, offset - 1],
            recv_sem=part_recv.at[s * tiles + tile, offset - 1],
            device_id=(other, block),
            device_id_type=mesh_id,
        )

    def align(s):
        row = shifts[pl.ds(s, 1), :]
        for top in range(0, chan_local, 8):
            column = to_sublanes(row, 8, top)
            chunks = [traces[s, top : top + 8, a * LANES : (a + 1) * LANES] for a in range(outer)]
            moved = move_earlier(chunks, column, 8)
            for a in range(outer):
                start = (s * tiles + a // 8) * unit_rows + (HALO + top) * 8 + a % 8
                ext[pl.ds(start, 8, stride=8), :] = moved[a]

    def send_halos(s):
        for tile in range(tiles):
            to_right, to_left = halo_copies(s * tiles + tile)
            pl.when(has_right)(to_right.start)
            pl.when(has_left)(to_left.start)

    small_loads[0].wait()
    trace_loads[0].wait()
    align(0)
    expected = has_left.astype(jnp.int32) + has_right.astype(jnp.int32) + (groups - 1)
    pl.semaphore_wait(barrier, expected)
    send_halos(0)

    def align_step(s, carry):
        align(s)
        send_halos(s)
        return carry

    for load in trace_loads[1:]:
        load.wait()
    lax.fori_loop(1, shot_local, align_step, 0)
    for load in small_loads[1:]:
        load.wait()
    table_hi[...] = table[...].astype(jnp.bfloat16)
    table_lo[...] = (table[...] - table_hi[...].astype(jnp.float32)).astype(jnp.bfloat16)

    def clear(first):
        def clear_step(unit, carry):
            rows = pl.ds(pl.multiple_of(unit * unit_rows + first, 8), halo_rows)
            ext[rows, :] = jnp.zeros((halo_rows, LANES), jnp.float32)
            return carry

        lax.fori_loop(0, shot_local * tiles, clear_step, 0)

    pl.when(jnp.logical_not(has_left))(lambda: clear(0))
    pl.when(jnp.logical_not(has_right))(lambda: clear(halo_rows + chan_local * 8))
    for c in range(chan_local):
        second[c * span : c * span + back, :] = jnp.zeros((back, LANES), jnp.float32)

    def forward(load, shot_id):
        values = real_dft([load(a) for a in range(outer)])
        for c in range(half):
            re, im = values[c]
            cos, sin = twist[0, c : c + 1, :], twist[1, c : c + 1, :]
            spec[shot_id, c, :, 0:LANES] = re * cos + im * sin
            spec[shot_id, c, :, LANES : 2 * LANES] = im * cos - re * sin
        padded = spec.shape[1]
        if padded > half:
            spec[shot_id, half:padded] = jnp.zeros((padded - half, rec, 2 * LANES), jnp.float32)
        flat = spec[shot_id].reshape(padded * rec, 2 * LANES)
        flat = split_dot(flat, table_hi[...], table_lo[...])
        spec[shot_id] = flat.reshape(padded, rec, 2 * LANES)

    edge_low = jnp.broadcast_to(has_left, (8, LANES))
    edge_high = jnp.broadcast_to(has_right, (8, LANES))

    def drain_parts(s):
        for tile in range(tiles):
            for offset in range(1, groups):
                part_copy(s, tile, offset).wait_send()

    def clean_step(s, carry):
        shot_id = part * shot_local + s
        row = shifts[pl.ds(s, 1), :]
        moves = []
        for g in range(groups):
            column = to_sublanes(row, rec, g * rec)
            low = to_sublanes(lo_ref[...], rec, g * rec)
            high = to_sublanes(hi_ref[...], rec, g * rec)
            inside = ((low <= shot_id) & (high > shot_id)).astype(jnp.int32)
            inside = jnp.broadcast_to(inside, (rec, LANES)) == 1
            moves.append((whole_chunks(column, rec),) + rotate_index(column, -1, rec) + (inside,))

        def unit_step(tile, carry):
            unit = s * tiles + tile
            to_right, to_left = halo_copies(unit)
            pl.when(has_left)(to_right.wait_recv)
            pl.when(has_right)(to_left.wait_recv)
            base = unit * unit_rows

            def rows_at(j):
                return ext[pl.ds(pl.multiple_of(base + j * 8, 8), 8), :]

            rows = {j: rows_at(j) for j in range(chan_local + 2 * HALO)}
            centers = list(range(REACH, chan_local + 2 * HALO - REACH))
            found = median_rows(rows, centers)
            cleaned = {}
            for j in centers:
                value = rows[j] - found[j]
                if j < HALO:
                    value = jnp.where(edge_low, value, 0.0)
                elif j >= HALO + chan_local:
                    value = jnp.where(edge_high, value, 0.0)
                cleaned[j] = value
            centers = list(range(HALO, HALO + chan_local))
            found = median_rows(cleaned, centers)
            for j in centers:
                start = pl.multiple_of((j - HALO) * span + back + tile * 8, 8)
                second[pl.ds(start, 8), :] = cleaned[j] - found[j]

            for g in range(groups):
                chosen, index, crossed, inside = moves[g]
                chunks = [
                    second[pl.ds(g * rec * span + tile * 8 + a, rec, stride=span), :]
                    for a in range(back + 8)
                ]
                for a, value in enumerate(move_later(chunks, chosen, index, crossed)):
                    up[s, g, tile * 8 + a] = jnp.where(inside, value, 0.0)
            for offset in range(1, groups):
                part_copy(s, tile, offset).start()
            return carry

        lax.fori_loop(0, tiles, unit_step, 0)
        forward(lambda a: up[s, part, a], shot_id)

        @pl.when(s > 0)
        def _():
            arrive(s - 1)

        return carry

    def arrive(s):
        for offset in range(1, groups):
            for tile in range(tiles):
                part_copy(s, tile, offset).wait_recv()
            source = lax.rem(part + groups - offset, groups)
            shot_id = source * shot_local + s
            forward(lambda a: got[shot_id, a], shot_id)

    lax.fori_loop(0, shot_local, clean_step, 0)

    def drain_step(unit, carry):
        to_right, to_left = halo_copies(unit)
        pl.when(has_right)(to_right.wait_send)
        pl.when(has_left)(to_left.wait_send)
        return carry

    lax.fori_loop(0, shot_local * tiles, drain_step, 0)
    for s in range(shot_local - 1):
        drain_parts(s)
    arrive(shot_local - 1)

    band = jnp.broadcast_to(to_sublanes(band_ref[...], rec, part * rec), (rec, LANES))
    lane_ids = lax.broadcasted_iota(jnp.int32, (rec, LANES), 1)

    for c in range(half):
        frequency = lane_ids * outer + c
        freq_abs = jnp.minimum(frequency, length - frequency)
        values = [
            (spec[s, c, :, 0:LANES], spec[s, c, :, LANES : 2 * LANES]) for s in range(shots)
        ]
        waves = complex_dft(values, -1)
        kept = []
        for k in range(shots):
            keep = min(k, shots - k) * band <= freq_abs
            kept.append((jnp.where(keep, waves[k][0], 0.0), jnp.where(keep, waves[k][1], 0.0)))
        values = complex_dft(kept, 1)
        for s in range(shots):
            spec[s, c, :, 0:LANES] = values[s][0]
            spec[s, c, :, LANES : 2 * LANES] = -values[s][1]

    padded = spec.shape[1]
    batch = shots // 2
    for first in range(0, shots, batch):
        flat = spec[first : first + batch].reshape(batch * padded * rec, 2 * LANES)
        flat = split_dot(flat, table_hi[...], table_lo[...])
        spec[first : first + batch] = flat.reshape(batch, padded, rec, 2 * LANES)

    def out_copy(s):
        return pltpu.make_async_copy(out.at[s], out_hbm.at[s], out_sem.at[s])

    def back(s):
        values = []
        for c in range(half):
            re, minus = spec[s, c, :, 0:LANES], spec[s, c, :, LANES : 2 * LANES]
            cos, sin = twist[0, c : c + 1, :], twist[1, c : c + 1, :]
            values.append((re * cos + minus * sin, re * sin - minus * cos))
        for a, value in enumerate(real_inverse(values, outer)):
            out[s, :, a * LANES : (a + 1) * LANES] = value
        out_copy(s).start()

    def back_step(pair, carry):
        back(2 * pair)
        back(2 * pair + 1)
        return carry

    lax.fori_loop(0, shots // 2, back_step, 0)

    drain_parts(shot_local - 1)
    for s in range(shots):
        out_copy(s).wait()


def tables(length):
    outer = length // LANES
    ids = np.arange(LANES)
    angles = 2.0 * np.pi * (np.outer(ids, ids) % LANES) / LANES
    cos, sin = np.cos(angles), np.sin(angles)
    table = np.block([[cos, -sin], [sin, cos]]).astype(np.float32)
    product = np.outer(np.arange(outer // 2 + 1), ids) % length
    angles = 2.0 * np.pi * product / length
    twist = np.stack([np.cos(angles), np.sin(angles)])
    return table, twist.astype(np.float32)


def local(groups, blocks, traces, shifts, aperture_lo, aperture_hi, dip_band):
    shot_local, chan_local, length = traces.shape
    outer = length // LANES
    rec = chan_local // groups
    shots = groups * shot_local
    padded = outer // 2 + 2
    constants = [jnp.asarray(item) for item in tables(length)]
    operands = [
        traces, shifts, aperture_lo[None, :], aperture_hi[None, :], dip_band[None, :], *constants
    ]
    others = max(groups - 1, 1)
    units = shot_local * (outer // 8)
    summed = pl.pallas_call(
        functools.partial(kernel, groups, blocks),
        out_shape=jax.ShapeDtypeStruct((shots, rec, length), jnp.float32),
        in_specs=[pl.BlockSpec(memory_space=pltpu.HBM)] * len(operands),
        out_specs=pl.BlockSpec(memory_space=pltpu.HBM),
        scratch_shapes=[pltpu.VMEM(item.shape, item.dtype) for item in operands] + [
            pltpu.VMEM((shot_local * (chan_local + 2 * HALO) * outer, LANES), jnp.float32),
            pltpu.VMEM((chan_local * (outer + outer // 4), LANES), jnp.float32),
            pltpu.VMEM((shot_local, groups, outer, rec, LANES), jnp.float32),
            pltpu.VMEM((shots, outer, rec, LANES), jnp.float32),
            pltpu.VMEM((shots, padded, rec, 2 * LANES), jnp.float32),
            pltpu.VMEM((shots, rec, length), jnp.float32),
            pltpu.VMEM((2 * LANES, 2 * LANES), jnp.bfloat16),
            pltpu.VMEM((2 * LANES, 2 * LANES), jnp.bfloat16),
            pltpu.SemaphoreType.DMA((units, 2)),
            pltpu.SemaphoreType.DMA((units, 2)),
            pltpu.SemaphoreType.DMA((units, others)),
            pltpu.SemaphoreType.DMA((units, others)),
            pltpu.SemaphoreType.DMA((shot_local,)),
            pltpu.SemaphoreType.DMA((len(operands) - 1,)),
            pltpu.SemaphoreType.DMA((shots,)),
        ],
        compiler_params=pltpu.CompilerParams(
            collective_id=0, has_side_effects=True, vmem_limit_bytes=60 * 1024 * 1024
        ),
    )(*operands)
    return summed * np.float32(1.0 / (shots * length))


def solution(mesh):
    return jax.shard_map(
        functools.partial(local, mesh.shape["shot"], mesh.shape["chan"]),
        mesh=mesh,
        in_specs=(P("shot", "chan", None), P("shot", "chan"), P("chan"), P("chan"), P("chan")),
        out_specs=P(None, ("chan", "shot"), None),
        check_vma=False,
    )
```

```python
import functools
import math

import jax
import jax.numpy as jnp
import numpy as np
from jax import lax
from jax.experimental import pallas as pl
from jax.experimental.pallas import tpu as pltpu
from jax.sharding import PartitionSpec as P

LANES = 128
REACH = 5
HALO = 2 * REACH


def sort_two(a, b):
    return jnp.minimum(a, b), jnp.maximum(a, b)


def median_rows(rows, centers):
    pairs = {}
    fours = {}
    results = {}

    def pair(at):
        if at not in pairs:
            pairs[at] = sort_two(rows[at], rows[at + 1])
        return pairs[at]

    def four(at):
        if at not in fours:
            a, b = pair(at)
            c, d = pair(at + 2)
            low, mid_a = sort_two(a, c)
            mid_b, high = sort_two(b, d)
            mid_a, mid_b = sort_two(mid_a, mid_b)
            fours[at] = (low, mid_a, mid_b, high)
        return fours[at]

    def middle_two(core, extra):
        a, b, c, d = core
        p, q = extra
        low = jnp.minimum(c, jnp.minimum(jnp.maximum(b, p), jnp.maximum(a, q)))
        high = jnp.maximum(b, jnp.maximum(jnp.minimum(d, p), jnp.minimum(c, q)))
        return low, high

    def clamp(value, ends):
        return jnp.maximum(ends[0], jnp.minimum(value, ends[1]))

    last = centers[-1]
    for c in centers[::4]:
        x, y = four(c - 2), four(c + 2)
        low = [jnp.minimum(x[i], y[3 - i]) for i in range(4)]
        high = [jnp.maximum(x[i], y[3 - i]) for i in range(4)]
        core = sort_two(jnp.maximum(low[0], low[2]), jnp.maximum(low[1], low[3])) + sort_two(
            jnp.minimum(high[0], high[2]), jnp.minimum(high[1], high[3])
        )
        ends = middle_two(core, pair(c - 4))
        results[c] = clamp(rows[c - 5], ends)
        results[c + 1] = clamp(rows[c + 6], ends)
        if c + 2 <= last:
            ends = middle_two(core, pair(c + 6))
            results[c + 2] = clamp(rows[c - 3], ends)
            results[c + 3] = clamp(rows[c + 8], ends)
    return results


def turn(value, angle_index, size, sign):
    re, im = value
    angle_index = angle_index % size
    if angle_index == 0:
        return value
    if 4 * angle_index == size:
        return (-im, re) if sign > 0 else (im, -re)
    if 2 * angle_index == size:
        return (-re, -im)
    angle = 2.0 * math.pi * angle_index / size
    cos, sin = math.cos(angle), sign * math.sin(angle)
    if 8 * angle_index == size:
        return ((re - im) * cos, (re + im) * cos) if sign > 0 else ((re + im) * cos, (im - re) * cos)
    return (re * cos - im * sin, re * sin + im * cos)


def add(a, b):
    return (a[0] + b[0], a[1] + b[1])


def sub(a, b):
    return (a[0] - b[0], a[1] - b[1])


def conj(a):
    return (a[0], -a[1])


def complex_dft(values, sign):
    size = len(values)
    if size == 1:
        return values
    even = complex_dft(values[0::2], sign)
    odd = complex_dft(values[1::2], sign)
    odd = [turn(odd[k], k, size, sign) for k in range(size // 2)]
    return [add(even[k], odd[k]) for k in range(size // 2)] + [
        sub(even[k], odd[k]) for k in range(size // 2)
    ]


def real_dft(values):
    size = len(values)
    if size == 2:
        zero = jnp.zeros_like(values[0])
        return [(values[0] + values[1], zero), (values[0] - values[1], zero)]
    even, odd = real_dft(values[0::2]), real_dft(values[1::2])
    half = size // 2
    zero = jnp.zeros_like(values[0])
    result = [None] * (half + 1)
    result[0] = (even[0][0] + odd[0][0], zero)
    result[half] = (even[0][0] - odd[0][0], zero)
    for k in range(1, half // 2 + 1):
        if 2 * k == half:
            result[k] = (even[k][0], -odd[k][0])
        else:
            moved = turn(odd[k], k, size, -1)
            result[k] = add(even[k], moved)
            result[half - k] = conj(sub(even[k], moved))
    return result


def real_inverse(values, size):
    half = size // 2
    if size == 2:
        a, b = values[0][0], values[1][0]
        return [a + b, a - b]
    even, odd = [], []
    for k in range(half // 2 + 1):
        if k == 0:
            even.append((values[0][0] + values[half][0], None))
            odd.append((values[0][0] - values[half][0], None))
        elif 2 * k == half:
            even.append((2.0 * values[k][0], None))
            odd.append((-2.0 * values[k][1], None))
        else:
            other = conj(values[half - k])
            even.append(add(values[k], other))
            odd.append(turn(sub(values[k], other), k, size, 1))
    first, second = real_inverse(even, half), real_inverse(odd, half)
    return [item for both in zip(first, second) for item in both]


def split_dot(x, high_table, low_table):
    high = x.astype(jnp.bfloat16)
    low = (x - high.astype(jnp.float32)).astype(jnp.bfloat16)

    def dot(a, b):
        return jnp.dot(a, b, preferred_element_type=jnp.float32)

    return dot(high, high_table) + (dot(low, high_table) + dot(high, low_table))


def to_sublanes(row, count, start):
    size = row.shape[1]
    row_ids = lax.broadcasted_iota(jnp.int32, (count, size), 0)
    col_ids = lax.broadcasted_iota(jnp.int32, (count, size), 1)
    spread = jnp.broadcast_to(row.astype(jnp.float32), (count, size))
    picked = jnp.where(col_ids == row_ids + start, spread, 0.0)
    return jnp.sum(picked, axis=1, keepdims=True).astype(jnp.int32)


def kernel(
    groups, blocks,
    traces_hbm, *rest,
):
    small_hbm, out_hbm, scratch = rest[:6], rest[6], rest[7:]
    traces, small, scratch = scratch[0], scratch[1:7], scratch[7:]
    shifts, lo_ref, hi_ref, band_ref, table, twist = small
    ext, second, up, got, spec, out, table_hi, table_lo, transit = scratch[:9]
    halo_send, halo_recv, part_send, part_recv, load_sem, small_sem, out_sem, transit_send, transit_recv = scratch[9:]
    shot_local, chan_local, length = traces.shape
    outer = length // LANES
    half = outer // 2 + 1
    rec = chan_local // groups
    shots = groups * shot_local
    tiles = outer // 8
    back = outer // 4
    span = outer + back
    unit_rows = (chan_local + 2 * HALO) * 8
    halo_rows = HALO * 8
    part = lax.axis_index("shot")
    block = lax.axis_index("chan")
    mesh_id = pl.DeviceIdType.MESH
    has_left = block > 0
    has_right = block < blocks - 1
    left = jnp.maximum(block - 1, 0)
    right = jnp.minimum(block + 1, blocks - 1)
    q_bits = max((length // 4 // LANES - 1).bit_length(), 0)

    small_loads = [
        pltpu.make_async_copy(small_hbm[i], small[i], small_sem.at[i]) for i in range(len(small))
    ]
    trace_loads = [
        pltpu.make_async_copy(traces_hbm.at[s], traces.at[s], load_sem.at[s]) for s in range(shot_local)
    ]
    small_loads[0].start()
    for load in trace_loads + small_loads[1:]:
        load.start()

    planes = blocks // 4
    relayed = groups == 2 and blocks % 4 == 0 and planes > 1 and tiles % planes == 0
    plane, place = block // 4, block % 4
    is_first = (place == 0).astype(jnp.int32)
    is_last = (place == 3).astype(jnp.int32)
    is_end = place % 3 == 0
    left_share = is_first * plane * (tiles // planes)
    right_share = is_last * (planes - 1 - plane) * (tiles // planes)
    transit_share = (is_last * plane + is_first * (planes - 1 - plane)) * (tiles // planes)
    corner = block + 3 * is_first - 3 * is_last
    onward = jnp.minimum(jnp.maximum(block + 4 * is_first - 4 * is_last, 0), blocks - 1)
    has_next = is_end & (block + 4 < blocks)
    has_before = is_end & (block >= 4)

    barrier = pltpu.get_barrier_semaphore()

    if relayed:
        for there, other in (
            (is_end, corner),
            (has_next, jnp.minimum(block + 4, blocks - 1)),
            (has_before, jnp.maximum(block - 4, 0)),
        ):
            @pl.when(there)
            def _():
                pl.semaphore_signal(barrier, inc=1, device_id=(part, other), device_id_type=mesh_id)

    @pl.when(has_left)
    def _():
        pl.semaphore_signal(barrier, inc=1, device_id=(part, left), device_id_type=mesh_id)

    @pl.when(has_right)
    def _():
        pl.semaphore_signal(barrier, inc=1, device_id=(part, right), device_id_type=mesh_id)

    for offset in range(1, groups):
        pl.semaphore_signal(
            barrier, inc=1, device_id=(lax.rem(part + offset, groups), block), device_id_type=mesh_id
        )

    def rotate_index(column, sign, rows):
        lanes = lax.broadcasted_iota(jnp.int32, (rows, LANES), 1)
        low = jnp.broadcast_to(column & (LANES - 1), (rows, LANES))
        if sign > 0:
            place = lanes + low
            return place & (LANES - 1), place >= LANES
        place = lanes - low
        return place & (LANES - 1), place < 0

    def whole_chunks(column, rows):
        return [
            jnp.broadcast_to((column >> (7 + bit)) & 1, (rows, LANES)) == 1 for bit in range(q_bits)
        ]

    def move_earlier(chunks, column, rows):
        index, crossed = rotate_index(column, 1, rows)
        zero = jnp.zeros((rows, LANES), jnp.float32)
        turned = [jnp.take_along_axis(chunk, index, axis=1) for chunk in chunks]

        def at(items, place):
            return items[place] if place < outer else zero

        moved = [jnp.where(crossed, at(turned, a + 1), turned[a]) for a in range(outer)]
        for bit, chosen in enumerate(whole_chunks(column, rows)):
            moved = [jnp.where(chosen, at(moved, a + (1 << bit)), moved[a]) for a in range(outer)]
        return moved

    def move_later(chunks, chosen, index, crossed):
        moved = dict(enumerate(chunks))
        first = back + 8 - len(chunks)
        for bit in reversed(range(q_bits)):
            first += 1 << bit
            moved = {
                a: jnp.where(chosen[bit], moved[a - (1 << bit)], moved[a])
                for a in range(first, back + 8)
            }
        turned = {a: jnp.take_along_axis(moved[a], index, axis=1) for a in range(back - 1, back + 8)}
        return [jnp.where(crossed, turned[a - 1], turned[a]) for a in range(back, back + 8)]

    def halo_copies(unit):
        base = pl.multiple_of(unit * unit_rows, 8)
        to_right = pltpu.make_async_remote_copy(
            src_ref=ext.at[pl.ds(base + chan_local * 8, halo_rows)],
            dst_ref=ext.at[pl.ds(base, halo_rows)],
            send_sem=halo_send.at[unit, 0],
            recv_sem=halo_recv.at[unit, 0],
            device_id=(part, right),
            device_id_type=mesh_id,
        )
        to_left = pltpu.make_async_remote_copy(
            src_ref=ext.at[pl.ds(base + halo_rows, halo_rows)],
            dst_ref=ext.at[pl.ds(base + halo_rows + chan_local * 8, halo_rows)],
            send_sem=halo_send.at[unit, 1],
            recv_sem=halo_recv.at[unit, 1],
            device_id=(part, left),
            device_id_type=mesh_id,
        )
        return to_right, to_left

    def corner_copy(unit, side):
        base = pl.multiple_of(unit * unit_rows, 8)
        start = base + chan_local * 8 if side == 0 else base + halo_rows
        return pltpu.make_async_remote_copy(
            src_ref=ext.at[pl.ds(start, halo_rows)],
            dst_ref=transit.at[unit],
            send_sem=halo_send.at[unit, side],
            recv_sem=transit_recv.at[unit],
            device_id=(part, corner),
            device_id_type=mesh_id,
        )

    def onward_copy(unit):
        start = unit * unit_rows + is_last * (halo_rows + chan_local * 8)
        return pltpu.make_async_remote_copy(
            src_ref=transit.at[unit],
            dst_ref=ext.at[pl.ds(pl.multiple_of(start, 8), halo_rows)],
            send_sem=transit_send.at[unit],
            recv_sem=halo_recv.at[unit, is_last],
            device_id=(part, onward),
            device_id_type=mesh_id,
        )

    def part_copy(s, tile, offset):
        other = lax.rem(part + offset, groups)
        rows = pl.ds(pl.multiple_of(tile * 8, 8), 8)
        return pltpu.make_async_remote_copy(
            src_ref=up.at[s, other, rows],
            dst_ref=got.at[part * shot_local + s, rows],
            send_sem=part_send.at[s * tiles + tile, offset - 1],
            recv_sem=part_recv.at[s * tiles + tile, offset - 1],
            device_id=(other, block),
            device_id_type=mesh_id,
        )

    def align(s):
        row = shifts[pl.ds(s, 1), :]
        for top in range(0, chan_local, 8):
            column = to_sublanes(row, 8, top)
            chunks = [traces[s, top : top + 8, a * LANES : (a + 1) * LANES] for a in range(outer)]
            moved = move_earlier(chunks, column, 8)
            for a in range(outer):
                start = (s * tiles + a // 8) * unit_rows + (HALO + top) * 8 + a % 8
                ext[pl.ds(start, 8, stride=8), :] = moved[a]

    def send_halos(s):
        for tile in range(tiles):
            to_right, to_left = halo_copies(s * tiles + tile)
            if relayed:
                pl.when(has_right & (tile >= right_share))(to_right.start)
                pl.when(has_left & (tile >= left_share))(to_left.start)
                pl.when(has_right & (tile < right_share))(corner_copy(s * tiles + tile, 0).start)
                pl.when(has_left & (tile < left_share))(corner_copy(s * tiles + tile, 1).start)
            else:
                pl.when(has_right)(to_right.start)
                pl.when(has_left)(to_left.start)

    small_loads[0].wait()
    trace_loads[0].wait()
    align(0)
    expected = has_left.astype(jnp.int32) + has_right.astype(jnp.int32) + (groups - 1)
    if relayed:
        for there in (is_end, has_next, has_before):
            expected = expected + there.astype(jnp.int32)
    pl.semaphore_wait(barrier, expected)
    send_halos(0)

    def align_step(s, carry):
        align(s)
        send_halos(s)
        return carry

    for load in trace_loads[1:]:
        load.wait()
    lax.fori_loop(1, shot_local, align_step, 0)
    for load in small_loads[1:]:
        load.wait()
    table_hi[...] = table[...].astype(jnp.bfloat16)
    table_lo[...] = (table[...] - table_hi[...].astype(jnp.float32)).astype(jnp.bfloat16)

    def clear(first):
        def clear_step(unit, carry):
            rows = pl.ds(pl.multiple_of(unit * unit_rows + first, 8), halo_rows)
            ext[rows, :] = jnp.zeros((halo_rows, LANES), jnp.float32)
            return carry

        lax.fori_loop(0, shot_local * tiles, clear_step, 0)

    pl.when(jnp.logical_not(has_left))(lambda: clear(0))
    pl.when(jnp.logical_not(has_right))(lambda: clear(halo_rows + chan_local * 8))
    for c in range(chan_local):
        second[c * span : c * span + back, :] = jnp.zeros((back, LANES), jnp.float32)

    def forward(load, shot_id):
        values = real_dft([load(a) for a in range(outer)])
        for c in range(half):
            re, im = values[c]
            cos, sin = twist[0, c : c + 1, :], twist[1, c : c + 1, :]
            spec[shot_id, c, :, 0:LANES] = re * cos + im * sin
            spec[shot_id, c, :, LANES : 2 * LANES] = im * cos - re * sin
        padded = spec.shape[1]
        if padded > half:
            spec[shot_id, half:padded] = jnp.zeros((padded - half, rec, 2 * LANES), jnp.float32)
        flat = spec[shot_id].reshape(padded * rec, 2 * LANES)
        flat = split_dot(flat, table_hi[...], table_lo[...])
        spec[shot_id] = flat.reshape(padded, rec, 2 * LANES)

    edge_low = jnp.broadcast_to(has_left, (8, LANES))
    edge_high = jnp.broadcast_to(has_right, (8, LANES))

    def drain_parts(s):
        for tile in range(tiles):
            for offset in range(1, groups):
                part_copy(s, tile, offset).wait_send()

    def clean_step(s, carry):
        shot_id = part * shot_local + s
        row = shifts[pl.ds(s, 1), :]
        moves = []
        for g in range(groups):
            column = to_sublanes(row, rec, g * rec)
            low = to_sublanes(lo_ref[...], rec, g * rec)
            high = to_sublanes(hi_ref[...], rec, g * rec)
            inside = ((low <= shot_id) & (high > shot_id)).astype(jnp.int32)
            inside = jnp.broadcast_to(inside, (rec, LANES)) == 1
            moves.append((whole_chunks(column, rec),) + rotate_index(column, -1, rec) + (inside,))

        def unit_step(tile, carry):
            unit = s * tiles + tile
            if relayed:
                @pl.when(tile < transit_share)
                def _():
                    moving = onward_copy(unit)
                    corner_copy(unit, 0).wait_recv()
                    moving.start()

            to_right, to_left = halo_copies(unit)
            pl.when(has_left)(to_right.wait_recv)
            pl.when(has_right)(to_left.wait_recv)
            base = unit * unit_rows

            def rows_at(j):
                return ext[pl.ds(pl.multiple_of(base + j * 8, 8), 8), :]

            rows = {j: rows_at(j) for j in range(chan_local + 2 * HALO)}
            centers = list(range(REACH, chan_local + 2 * HALO - REACH))
            found = median_rows(rows, centers)
            cleaned = {}
            for j in centers:
                value = rows[j] - found[j]
                if j < HALO:
                    value = jnp.where(edge_low, value, 0.0)
                elif j >= HALO + chan_local:
                    value = jnp.where(edge_high, value, 0.0)
                cleaned[j] = value
            centers = list(range(HALO, HALO + chan_local))
            found = median_rows(cleaned, centers)
            for j in centers:
                start = pl.multiple_of((j - HALO) * span + back + tile * 8, 8)
                second[pl.ds(start, 8), :] = cleaned[j] - found[j]

            for g in range(groups):
                chosen, index, crossed, inside = moves[g]
                chunks = [
                    second[pl.ds(g * rec * span + tile * 8 + a, rec, stride=span), :]
                    for a in range(back + 8)
                ]
                for a, value in enumerate(move_later(chunks, chosen, index, crossed)):
                    up[s, g, tile * 8 + a] = jnp.where(inside, value, 0.0)
            for offset in range(1, groups):
                part_copy(s, tile, offset).start()
            return carry

        lax.fori_loop(0, tiles, unit_step, 0)
        forward(lambda a: up[s, part, a], shot_id)

        @pl.when(s > 0)
        def _():
            arrive(s - 1)

        return carry

    def arrive(s):
        for offset in range(1, groups):
            for tile in range(tiles):
                part_copy(s, tile, offset).wait_recv()
            source = lax.rem(part + groups - offset, groups)
            shot_id = source * shot_local + s
            forward(lambda a: got[shot_id, a], shot_id)

    lax.fori_loop(0, shot_local, clean_step, 0)

    def drain_step(unit, carry):
        to_right, to_left = halo_copies(unit)
        pl.when(has_right)(to_right.wait_send)
        pl.when(has_left)(to_left.wait_send)
        if relayed:
            pl.when(unit % tiles < transit_share)(onward_copy(unit).wait_send)
        return carry

    lax.fori_loop(0, shot_local * tiles, drain_step, 0)
    for s in range(shot_local - 1):
        drain_parts(s)
    arrive(shot_local - 1)

    band = jnp.broadcast_to(to_sublanes(band_ref[...], rec, part * rec), (rec, LANES))
    lane_ids = lax.broadcasted_iota(jnp.int32, (rec, LANES), 1)

    for c in range(half):
        frequency = lane_ids * outer + c
        freq_abs = jnp.minimum(frequency, length - frequency)
        values = [
            (spec[s, c, :, 0:LANES], spec[s, c, :, LANES : 2 * LANES]) for s in range(shots)
        ]
        waves = complex_dft(values, -1)
        kept = []
        for k in range(shots):
            keep = min(k, shots - k) * band <= freq_abs
            kept.append((jnp.where(keep, waves[k][0], 0.0), jnp.where(keep, waves[k][1], 0.0)))
        values = complex_dft(kept, 1)
        for s in range(shots):
            spec[s, c, :, 0:LANES] = values[s][0]
            spec[s, c, :, LANES : 2 * LANES] = -values[s][1]

    padded = spec.shape[1]
    batch = shots // 2
    for first in range(0, shots, batch):
        flat = spec[first : first + batch].reshape(batch * padded * rec, 2 * LANES)
        flat = split_dot(flat, table_hi[...], table_lo[...])
        spec[first : first + batch] = flat.reshape(batch, padded, rec, 2 * LANES)

    def out_copy(s):
        return pltpu.make_async_copy(out.at[s], out_hbm.at[s], out_sem.at[s])

    def back(s):
        values = []
        for c in range(half):
            re, minus = spec[s, c, :, 0:LANES], spec[s, c, :, LANES : 2 * LANES]
            cos, sin = twist[0, c : c + 1, :], twist[1, c : c + 1, :]
            values.append((re * cos + minus * sin, re * sin - minus * cos))
        for a, value in enumerate(real_inverse(values, outer)):
            out[s, :, a * LANES : (a + 1) * LANES] = value
        out_copy(s).start()

    def back_step(pair, carry):
        back(2 * pair)
        back(2 * pair + 1)
        return carry

    lax.fori_loop(0, shots // 2, back_step, 0)

    drain_parts(shot_local - 1)
    for s in range(shots):
        out_copy(s).wait()


def tables(length):
    outer = length // LANES
    ids = np.arange(LANES)
    angles = 2.0 * np.pi * (np.outer(ids, ids) % LANES) / LANES
    cos, sin = np.cos(angles), np.sin(angles)
    table = np.block([[cos, -sin], [sin, cos]]).astype(np.float32)
    product = np.outer(np.arange(outer // 2 + 1), ids) % length
    angles = 2.0 * np.pi * product / length
    twist = np.stack([np.cos(angles), np.sin(angles)])
    return table, twist.astype(np.float32)


def local(groups, blocks, traces, shifts, aperture_lo, aperture_hi, dip_band):
    shot_local, chan_local, length = traces.shape
    outer = length // LANES
    rec = chan_local // groups
    shots = groups * shot_local
    padded = outer // 2 + 2
    constants = [jnp.asarray(item) for item in tables(length)]
    operands = [
        traces, shifts, aperture_lo[None, :], aperture_hi[None, :], dip_band[None, :], *constants
    ]
    others = max(groups - 1, 1)
    units = shot_local * (outer // 8)
    summed = pl.pallas_call(
        functools.partial(kernel, groups, blocks),
        out_shape=jax.ShapeDtypeStruct((shots, rec, length), jnp.float32),
        in_specs=[pl.BlockSpec(memory_space=pltpu.HBM)] * len(operands),
        out_specs=pl.BlockSpec(memory_space=pltpu.HBM),
        scratch_shapes=[pltpu.VMEM(item.shape, item.dtype) for item in operands] + [
            pltpu.VMEM((shot_local * (chan_local + 2 * HALO) * outer, LANES), jnp.float32),
            pltpu.VMEM((chan_local * (outer + outer // 4), LANES), jnp.float32),
            pltpu.VMEM((shot_local, groups, outer, rec, LANES), jnp.float32),
            pltpu.VMEM((shots, outer, rec, LANES), jnp.float32),
            pltpu.VMEM((shots, padded, rec, 2 * LANES), jnp.float32),
            pltpu.VMEM((shots, rec, length), jnp.float32),
            pltpu.VMEM((2 * LANES, 2 * LANES), jnp.bfloat16),
            pltpu.VMEM((2 * LANES, 2 * LANES), jnp.bfloat16),
            pltpu.VMEM((units, HALO * 8, LANES), jnp.float32),
            pltpu.SemaphoreType.DMA((units, 2)),
            pltpu.SemaphoreType.DMA((units, 2)),
            pltpu.SemaphoreType.DMA((units, others)),
            pltpu.SemaphoreType.DMA((units, others)),
            pltpu.SemaphoreType.DMA((shot_local,)),
            pltpu.SemaphoreType.DMA((len(operands) - 1,)),
            pltpu.SemaphoreType.DMA((shots,)),
            pltpu.SemaphoreType.DMA((units,)),
            pltpu.SemaphoreType.DMA((units,)),
        ],
        compiler_params=pltpu.CompilerParams(
            collective_id=0, has_side_effects=True, vmem_limit_bytes=60 * 1024 * 1024
        ),
    )(*operands)
    return summed * np.float32(1.0 / (shots * length))


def solution(mesh):
    return jax.shard_map(
        functools.partial(local, mesh.shape["shot"], mesh.shape["chan"]),
        mesh=mesh,
        in_specs=(P("shot", "chan", None), P("shot", "chan"), P("chan"), P("chan"), P("chan")),
        out_specs=P(None, ("chan", "shot"), None),
        check_vma=False,
    )
```

```python
import functools
import math

import jax
import jax.numpy as jnp
import numpy as np
from jax import lax
from jax.experimental import pallas as pl
from jax.experimental.pallas import tpu as pltpu
from jax.sharding import PartitionSpec as P

LANES = 128
REACH = 5
HALO = 2 * REACH


def sort_two(a, b):
    return jnp.minimum(a, b), jnp.maximum(a, b)


def median_rows(rows, centers):
    pairs = {}
    fours = {}
    results = {}

    def pair(at):
        if at not in pairs:
            pairs[at] = sort_two(rows[at], rows[at + 1])
        return pairs[at]

    def four(at):
        if at not in fours:
            a, b = pair(at)
            c, d = pair(at + 2)
            low, mid_a = sort_two(a, c)
            mid_b, high = sort_two(b, d)
            mid_a, mid_b = sort_two(mid_a, mid_b)
            fours[at] = (low, mid_a, mid_b, high)
        return fours[at]

    def middle_two(core, extra):
        a, b, c, d = core
        p, q = extra
        low = jnp.minimum(c, jnp.minimum(jnp.maximum(b, p), jnp.maximum(a, q)))
        high = jnp.maximum(b, jnp.maximum(jnp.minimum(d, p), jnp.minimum(c, q)))
        return low, high

    def clamp(value, ends):
        return jnp.maximum(ends[0], jnp.minimum(value, ends[1]))

    last = centers[-1]
    for c in centers[::4]:
        x, y = four(c - 2), four(c + 2)
        low = [jnp.minimum(x[i], y[3 - i]) for i in range(4)]
        high = [jnp.maximum(x[i], y[3 - i]) for i in range(4)]
        core = sort_two(jnp.maximum(low[0], low[2]), jnp.maximum(low[1], low[3])) + sort_two(
            jnp.minimum(high[0], high[2]), jnp.minimum(high[1], high[3])
        )
        ends = middle_two(core, pair(c - 4))
        results[c] = clamp(rows[c - 5], ends)
        results[c + 1] = clamp(rows[c + 6], ends)
        if c + 2 <= last:
            ends = middle_two(core, pair(c + 6))
            results[c + 2] = clamp(rows[c - 3], ends)
            results[c + 3] = clamp(rows[c + 8], ends)
    return results


def turn(value, angle_index, size, sign):
    re, im = value
    angle_index = angle_index % size
    if angle_index == 0:
        return value
    if 4 * angle_index == size:
        return (-im, re) if sign > 0 else (im, -re)
    if 2 * angle_index == size:
        return (-re, -im)
    angle = 2.0 * math.pi * angle_index / size
    cos, sin = math.cos(angle), sign * math.sin(angle)
    if 8 * angle_index == size:
        return ((re - im) * cos, (re + im) * cos) if sign > 0 else ((re + im) * cos, (im - re) * cos)
    return (re * cos - im * sin, re * sin + im * cos)


def add(a, b):
    return (a[0] + b[0], a[1] + b[1])


def sub(a, b):
    return (a[0] - b[0], a[1] - b[1])


def conj(a):
    return (a[0], -a[1])


def complex_dft(values, sign):
    size = len(values)
    if size == 1:
        return values
    even = complex_dft(values[0::2], sign)
    odd = complex_dft(values[1::2], sign)
    odd = [turn(odd[k], k, size, sign) for k in range(size // 2)]
    return [add(even[k], odd[k]) for k in range(size // 2)] + [
        sub(even[k], odd[k]) for k in range(size // 2)
    ]


def real_dft(values):
    size = len(values)
    if size == 2:
        zero = jnp.zeros_like(values[0])
        return [(values[0] + values[1], zero), (values[0] - values[1], zero)]
    even, odd = real_dft(values[0::2]), real_dft(values[1::2])
    half = size // 2
    zero = jnp.zeros_like(values[0])
    result = [None] * (half + 1)
    result[0] = (even[0][0] + odd[0][0], zero)
    result[half] = (even[0][0] - odd[0][0], zero)
    for k in range(1, half // 2 + 1):
        if 2 * k == half:
            result[k] = (even[k][0], -odd[k][0])
        else:
            moved = turn(odd[k], k, size, -1)
            result[k] = add(even[k], moved)
            result[half - k] = conj(sub(even[k], moved))
    return result


def real_inverse(values, size):
    half = size // 2
    if size == 2:
        a, b = values[0][0], values[1][0]
        return [a + b, a - b]
    even, odd = [], []
    for k in range(half // 2 + 1):
        if k == 0:
            even.append((values[0][0] + values[half][0], None))
            odd.append((values[0][0] - values[half][0], None))
        elif 2 * k == half:
            even.append((2.0 * values[k][0], None))
            odd.append((-2.0 * values[k][1], None))
        else:
            other = conj(values[half - k])
            even.append(add(values[k], other))
            odd.append(turn(sub(values[k], other), k, size, 1))
    first, second = real_inverse(even, half), real_inverse(odd, half)
    return [item for both in zip(first, second) for item in both]


def split_dot(x, high_table, low_table):
    high = x.astype(jnp.bfloat16)
    low = (x - high.astype(jnp.float32)).astype(jnp.bfloat16)

    def dot(a, b):
        return jnp.dot(a, b, preferred_element_type=jnp.float32)

    return dot(high, high_table) + (dot(low, high_table) + dot(high, low_table))


def to_sublanes(row, count, start):
    size = row.shape[1]
    row_ids = lax.broadcasted_iota(jnp.int32, (count, size), 0)
    col_ids = lax.broadcasted_iota(jnp.int32, (count, size), 1)
    spread = jnp.broadcast_to(row.astype(jnp.float32), (count, size))
    picked = jnp.where(col_ids == row_ids + start, spread, 0.0)
    return jnp.sum(picked, axis=1, keepdims=True).astype(jnp.int32)


def kernel(
    groups, blocks,
    traces_hbm, *rest,
):
    numbers_hbm, rows_hbm, out, scratch = rest[0], rest[1], rest[2], rest[3:]
    traces, small, scratch = scratch[0], scratch[1:4], scratch[4:]
    numbers, table, twist = small
    small_hbm = (
        numbers_hbm, rows_hbm.at[0 : 2 * LANES], rows_hbm.at[2 * LANES : 2 * LANES + twist.shape[0]],
    )
    ext, second, up, got, spec, table_hi, table_lo = scratch[:7]
    halo_send, halo_recv, part_send, part_recv, load_sem, small_sem = scratch[7:]
    shot_local, chan_local, length = traces.shape
    outer = length // LANES
    half = outer // 2 + 1
    rec = chan_local // groups
    shots = groups * shot_local
    tiles = outer // 8
    back = outer // 4
    span = outer + back
    unit_rows = (chan_local + 2 * HALO) * 8
    halo_rows = HALO * 8
    part = lax.axis_index("shot")
    block = lax.axis_index("chan")
    mesh_id = pl.DeviceIdType.MESH
    has_left = block > 0
    has_right = block < blocks - 1
    left = jnp.maximum(block - 1, 0)
    right = jnp.minimum(block + 1, blocks - 1)
    q_bits = max((length // 4 // LANES - 1).bit_length(), 0)

    small_loads = [
        pltpu.make_async_copy(small_hbm[i], small[i], small_sem.at[i]) for i in range(len(small))
    ]
    trace_loads = [
        pltpu.make_async_copy(traces_hbm.at[s], traces.at[s], load_sem.at[s]) for s in range(shot_local)
    ]
    small_loads[0].start()
    for load in trace_loads + small_loads[1:]:
        load.start()

    barrier = pltpu.get_barrier_semaphore()

    @pl.when(has_left)
    def _():
        pl.semaphore_signal(barrier, inc=1, device_id=(part, left), device_id_type=mesh_id)

    @pl.when(has_right)
    def _():
        pl.semaphore_signal(barrier, inc=1, device_id=(part, right), device_id_type=mesh_id)

    for offset in range(1, groups):
        pl.semaphore_signal(
            barrier, inc=1, device_id=(lax.rem(part + offset, groups), block), device_id_type=mesh_id
        )

    def rotate_index(column, sign, rows):
        lanes = lax.broadcasted_iota(jnp.int32, (rows, LANES), 1)
        low = jnp.broadcast_to(column & (LANES - 1), (rows, LANES))
        if sign > 0:
            place = lanes + low
            return place & (LANES - 1), place >= LANES
        place = lanes - low
        return place & (LANES - 1), place < 0

    def whole_chunks(column, rows):
        return [
            jnp.broadcast_to((column >> (7 + bit)) & 1, (rows, LANES)) == 1 for bit in range(q_bits)
        ]

    def move_earlier(chunks, column, rows):
        index, crossed = rotate_index(column, 1, rows)
        zero = jnp.zeros((rows, LANES), jnp.float32)
        turned = [jnp.take_along_axis(chunk, index, axis=1) for chunk in chunks]

        def at(items, place):
            return items[place] if place < outer else zero

        moved = [jnp.where(crossed, at(turned, a + 1), turned[a]) for a in range(outer)]
        for bit, chosen in enumerate(whole_chunks(column, rows)):
            moved = [jnp.where(chosen, at(moved, a + (1 << bit)), moved[a]) for a in range(outer)]
        return moved

    def move_later(chunks, chosen, index, crossed):
        moved = dict(enumerate(chunks))
        first = back + 8 - len(chunks)
        for bit in reversed(range(q_bits)):
            first += 1 << bit
            moved = {
                a: jnp.where(chosen[bit], moved[a - (1 << bit)], moved[a])
                for a in range(first, back + 8)
            }
        turned = {a: jnp.take_along_axis(moved[a], index, axis=1) for a in range(back - 1, back + 8)}
        return [jnp.where(crossed, turned[a - 1], turned[a]) for a in range(back, back + 8)]

    def halo_copies(unit):
        base = pl.multiple_of(unit * unit_rows, 8)
        to_right = pltpu.make_async_remote_copy(
            src_ref=ext.at[pl.ds(base + chan_local * 8, halo_rows)],
            dst_ref=ext.at[pl.ds(base, halo_rows)],
            send_sem=halo_send.at[unit, 0],
            recv_sem=halo_recv.at[unit, 0],
            device_id=(part, right),
            device_id_type=mesh_id,
        )
        to_left = pltpu.make_async_remote_copy(
            src_ref=ext.at[pl.ds(base + halo_rows, halo_rows)],
            dst_ref=ext.at[pl.ds(base + halo_rows + chan_local * 8, halo_rows)],
            send_sem=halo_send.at[unit, 1],
            recv_sem=halo_recv.at[unit, 1],
            device_id=(part, left),
            device_id_type=mesh_id,
        )
        return to_right, to_left

    def part_copy(s, tile, offset):
        other = lax.rem(part + offset, groups)
        rows = pl.ds(pl.multiple_of(tile * 8, 8), 8)
        return pltpu.make_async_remote_copy(
            src_ref=up.at[s, other, rows],
            dst_ref=got.at[part * shot_local + s, rows],
            send_sem=part_send.at[s * tiles + tile, offset - 1],
            recv_sem=part_recv.at[s * tiles + tile, offset - 1],
            device_id=(other, block),
            device_id_type=mesh_id,
        )

    def align(s):
        row = numbers[pl.ds(s, 1), :]
        for top in range(0, chan_local, 8):
            column = to_sublanes(row, 8, top)
            chunks = [traces[s, top : top + 8, a * LANES : (a + 1) * LANES] for a in range(outer)]
            moved = move_earlier(chunks, column, 8)
            for a in range(outer):
                start = (s * tiles + a // 8) * unit_rows + (HALO + top) * 8 + a % 8
                ext[pl.ds(start, 8, stride=8), :] = moved[a]

    def send_halos(s):
        for tile in range(tiles):
            to_right, to_left = halo_copies(s * tiles + tile)
            pl.when(has_right)(to_right.start)
            pl.when(has_left)(to_left.start)

    small_loads[0].wait()
    trace_loads[0].wait()
    align(0)
    expected = has_left.astype(jnp.int32) + has_right.astype(jnp.int32) + (groups - 1)
    pl.semaphore_wait(barrier, expected)
    send_halos(0)

    def align_step(s, carry):
        align(s)
        send_halos(s)
        return carry

    for load in trace_loads[1:]:
        load.wait()
    lax.fori_loop(1, shot_local, align_step, 0)
    for load in small_loads[1:]:
        load.wait()
    table_hi[...] = table[...].astype(jnp.bfloat16)
    table_lo[...] = (table[...] - table_hi[...].astype(jnp.float32)).astype(jnp.bfloat16)

    def clear(first):
        def clear_step(unit, carry):
            rows = pl.ds(pl.multiple_of(unit * unit_rows + first, 8), halo_rows)
            ext[rows, :] = jnp.zeros((halo_rows, LANES), jnp.float32)
            return carry

        lax.fori_loop(0, shot_local * tiles, clear_step, 0)

    pl.when(jnp.logical_not(has_left))(lambda: clear(0))
    pl.when(jnp.logical_not(has_right))(lambda: clear(halo_rows + chan_local * 8))
    for c in range(chan_local):
        second[c * span : c * span + back, :] = jnp.zeros((back, LANES), jnp.float32)

    def forward(load, shot_id):
        values = real_dft([load(a) for a in range(outer)])
        for c in range(half):
            re, im = values[c]
            cos, sin = twist[c : c + 1, 0:LANES], twist[c : c + 1, LANES : 2 * LANES]
            spec[shot_id, c, :, 0:LANES] = re * cos + im * sin
            spec[shot_id, c, :, LANES : 2 * LANES] = im * cos - re * sin
        padded = spec.shape[1]
        if padded > half:
            spec[shot_id, half:padded] = jnp.zeros((padded - half, rec, 2 * LANES), jnp.float32)
        flat = spec[shot_id].reshape(padded * rec, 2 * LANES)
        flat = split_dot(flat, table_hi[...], table_lo[...])
        spec[shot_id] = flat.reshape(padded, rec, 2 * LANES)

    edge_low = jnp.broadcast_to(has_left, (8, LANES))
    edge_high = jnp.broadcast_to(has_right, (8, LANES))

    def drain_parts(s):
        for tile in range(tiles):
            for offset in range(1, groups):
                part_copy(s, tile, offset).wait_send()

    def clean_step(s, carry):
        shot_id = part * shot_local + s
        row = numbers[pl.ds(s, 1), :]
        moves = []
        for g in range(groups):
            column = to_sublanes(row, rec, g * rec)
            low = to_sublanes(numbers[shot_local : shot_local + 1, :], rec, g * rec)
            high = to_sublanes(numbers[shot_local + 1 : shot_local + 2, :], rec, g * rec)
            inside = ((low <= shot_id) & (high > shot_id)).astype(jnp.int32)
            inside = jnp.broadcast_to(inside, (rec, LANES)) == 1
            moves.append((whole_chunks(column, rec),) + rotate_index(column, -1, rec) + (inside,))

        def unit_step(tile, carry):
            unit = s * tiles + tile
            to_right, to_left = halo_copies(unit)
            pl.when(has_left)(to_right.wait_recv)
            pl.when(has_right)(to_left.wait_recv)
            base = unit * unit_rows

            def rows_at(j):
                return ext[pl.ds(pl.multiple_of(base + j * 8, 8), 8), :]

            rows = {j: rows_at(j) for j in range(chan_local + 2 * HALO)}
            centers = list(range(REACH, chan_local + 2 * HALO - REACH))
            found = median_rows(rows, centers)
            cleaned = {}
            for j in centers:
                value = rows[j] - found[j]
                if j < HALO:
                    value = jnp.where(edge_low, value, 0.0)
                elif j >= HALO + chan_local:
                    value = jnp.where(edge_high, value, 0.0)
                cleaned[j] = value
            centers = list(range(HALO, HALO + chan_local))
            found = median_rows(cleaned, centers)
            for j in centers:
                start = pl.multiple_of((j - HALO) * span + back + tile * 8, 8)
                second[pl.ds(start, 8), :] = cleaned[j] - found[j]

            for g in range(groups):
                chosen, index, crossed, inside = moves[g]
                chunks = [
                    second[pl.ds(g * rec * span + tile * 8 + a, rec, stride=span), :]
                    for a in range(back + 8)
                ]
                for a, value in enumerate(move_later(chunks, chosen, index, crossed)):
                    up[s, g, tile * 8 + a] = jnp.where(inside, value, 0.0)
            for offset in range(1, groups):
                part_copy(s, tile, offset).start()
            return carry

        lax.fori_loop(0, tiles, unit_step, 0)
        forward(lambda a: up[s, part, a], shot_id)

        @pl.when(s > 0)
        def _():
            arrive(s - 1)

        return carry

    def arrive(s):
        for offset in range(1, groups):
            for tile in range(tiles):
                part_copy(s, tile, offset).wait_recv()
            source = lax.rem(part + groups - offset, groups)
            shot_id = source * shot_local + s
            forward(lambda a: got[shot_id, a], shot_id)

    lax.fori_loop(0, shot_local, clean_step, 0)

    def drain_step(unit, carry):
        to_right, to_left = halo_copies(unit)
        pl.when(has_right)(to_right.wait_send)
        pl.when(has_left)(to_left.wait_send)
        return carry

    lax.fori_loop(0, shot_local * tiles, drain_step, 0)
    for s in range(shot_local - 1):
        drain_parts(s)
    arrive(shot_local - 1)

    band = jnp.broadcast_to(to_sublanes(numbers[shot_local + 2 : shot_local + 3, :], rec, part * rec), (rec, LANES))
    lane_ids = lax.broadcasted_iota(jnp.int32, (rec, LANES), 1)

    for c in range(half):
        frequency = lane_ids * outer + c
        freq_abs = jnp.minimum(frequency, length - frequency)
        values = [
            (spec[s, c, :, 0:LANES], spec[s, c, :, LANES : 2 * LANES]) for s in range(shots)
        ]
        waves = complex_dft(values, -1)
        kept = []
        for k in range(shots):
            keep = min(k, shots - k) * band <= freq_abs
            kept.append((jnp.where(keep, waves[k][0], 0.0), jnp.where(keep, waves[k][1], 0.0)))
        values = complex_dft(kept, 1)
        for s in range(shots):
            spec[s, c, :, 0:LANES] = values[s][0]
            spec[s, c, :, LANES : 2 * LANES] = -values[s][1]

    padded = spec.shape[1]
    batch = shots // 2
    for first in range(0, shots, batch):
        flat = spec[first : first + batch].reshape(batch * padded * rec, 2 * LANES)
        flat = split_dot(flat, table_hi[...], table_lo[...])
        spec[first : first + batch] = flat.reshape(batch, padded, rec, 2 * LANES)

    def back(s):
        values = []
        for c in range(half):
            re, minus = spec[s, c, :, 0:LANES], spec[s, c, :, LANES : 2 * LANES]
            cos, sin = twist[c : c + 1, 0:LANES], twist[c : c + 1, LANES : 2 * LANES]
            values.append((re * cos + minus * sin, re * sin - minus * cos))
        for a, value in enumerate(real_inverse(values, outer)):
            out[s, :, a * LANES : (a + 1) * LANES] = value

    def back_step(pair, carry):
        back(2 * pair)
        back(2 * pair + 1)
        return carry

    lax.fori_loop(0, shots // 2, back_step, 0)

    drain_parts(shot_local - 1)


def tables(length):
    outer = length // LANES
    ids = np.arange(LANES)
    angles = 2.0 * np.pi * (np.outer(ids, ids) % LANES) / LANES
    cos, sin = np.cos(angles), np.sin(angles)
    table = np.block([[cos, -sin], [sin, cos]]).astype(np.float32)
    half = outer // 2 + 1
    angles = 2.0 * np.pi * (np.outer(np.arange(half), ids) % length) / length
    rows = np.zeros((16 * 2 * LANES, 2 * LANES), np.float32)
    rows[: 2 * LANES] = table
    rows[2 * LANES : 2 * LANES + half] = np.concatenate([np.cos(angles), np.sin(angles)], axis=1)
    return rows


def local(groups, blocks, traces, shifts, aperture_lo, aperture_hi, dip_band):
    shot_local, chan_local, length = traces.shape
    outer = length // LANES
    rec = chan_local // groups
    shots = groups * shot_local
    padded = outer // 2 + 2
    constants = jnp.asarray(tables(length))
    twist_rows = -(-(outer // 2 + 1) // 8) * 8
    numbers = jnp.concatenate(
        [shifts, aperture_lo[None, :], aperture_hi[None, :], dip_band[None, :]], axis=0
    )
    operands = [traces, numbers, constants]
    others = max(groups - 1, 1)
    units = shot_local * (outer // 8)
    summed = pl.pallas_call(
        functools.partial(kernel, groups, blocks),
        out_shape=jax.ShapeDtypeStruct((shots, rec, length), jnp.float32),
        in_specs=[pl.BlockSpec(memory_space=pltpu.HBM)] * len(operands),
        out_specs=pl.BlockSpec(memory_space=pltpu.VMEM),
        scratch_shapes=[pltpu.VMEM(item.shape, item.dtype) for item in operands[:-1]] + [
            pltpu.VMEM((2 * LANES, 2 * LANES), jnp.float32),
            pltpu.VMEM((twist_rows, 2 * LANES), jnp.float32),
            pltpu.VMEM((shot_local * (chan_local + 2 * HALO) * outer, LANES), jnp.float32),
            pltpu.VMEM((chan_local * (outer + outer // 4), LANES), jnp.float32),
            pltpu.VMEM((shot_local, groups, outer, rec, LANES), jnp.float32),
            pltpu.VMEM((shots, outer, rec, LANES), jnp.float32),
            pltpu.VMEM((shots, padded, rec, 2 * LANES), jnp.float32),
            pltpu.VMEM((2 * LANES, 2 * LANES), jnp.bfloat16),
            pltpu.VMEM((2 * LANES, 2 * LANES), jnp.bfloat16),
            pltpu.SemaphoreType.DMA((units, 2)),
            pltpu.SemaphoreType.DMA((units, 2)),
            pltpu.SemaphoreType.DMA((units, others)),
            pltpu.SemaphoreType.DMA((units, others)),
            pltpu.SemaphoreType.DMA((shot_local,)),
            pltpu.SemaphoreType.DMA((len(operands),)),
        ],
        compiler_params=pltpu.CompilerParams(
            collective_id=0, has_side_effects=True, vmem_limit_bytes=52 * 1024 * 1024
        ),
    )(*operands)
    return summed * np.float32(1.0 / (shots * length))


def solution(mesh):
    return jax.shard_map(
        functools.partial(local, mesh.shape["shot"], mesh.shape["chan"]),
        mesh=mesh,
        in_specs=(P("shot", "chan", None), P("shot", "chan"), P("chan"), P("chan"), P("chan")),
        out_specs=P(None, ("chan", "shot"), None),
        check_vma=False,
    )
```

```python
import functools
import math

import jax
import jax.numpy as jnp
import numpy as np
from jax import lax
from jax.experimental import pallas as pl
from jax.experimental.pallas import tpu as pltpu
from jax.sharding import PartitionSpec as P

LANES = 128
REACH = 5
HALO = 2 * REACH


def sort_two(a, b):
    return jnp.minimum(a, b), jnp.maximum(a, b)


def median_rows(rows, centers):
    pairs = {}
    fours = {}
    results = {}

    def pair(at):
        if at not in pairs:
            pairs[at] = sort_two(rows[at], rows[at + 1])
        return pairs[at]

    def four(at):
        if at not in fours:
            a, b = pair(at)
            c, d = pair(at + 2)
            low, mid_a = sort_two(a, c)
            mid_b, high = sort_two(b, d)
            mid_a, mid_b = sort_two(mid_a, mid_b)
            fours[at] = (low, mid_a, mid_b, high)
        return fours[at]

    def middle_two(core, extra):
        a, b, c, d = core
        p, q = extra
        low = jnp.minimum(c, jnp.minimum(jnp.maximum(b, p), jnp.maximum(a, q)))
        high = jnp.maximum(b, jnp.maximum(jnp.minimum(d, p), jnp.minimum(c, q)))
        return low, high

    def clamp(value, ends):
        return jnp.maximum(ends[0], jnp.minimum(value, ends[1]))

    last = centers[-1]
    for c in centers[::4]:
        x, y = four(c - 2), four(c + 2)
        low = [jnp.minimum(x[i], y[3 - i]) for i in range(4)]
        high = [jnp.maximum(x[i], y[3 - i]) for i in range(4)]
        core = sort_two(jnp.maximum(low[0], low[2]), jnp.maximum(low[1], low[3])) + sort_two(
            jnp.minimum(high[0], high[2]), jnp.minimum(high[1], high[3])
        )
        ends = middle_two(core, pair(c - 4))
        results[c] = clamp(rows[c - 5], ends)
        results[c + 1] = clamp(rows[c + 6], ends)
        if c + 2 <= last:
            ends = middle_two(core, pair(c + 6))
            results[c + 2] = clamp(rows[c - 3], ends)
            results[c + 3] = clamp(rows[c + 8], ends)
    return results


def turn(value, angle_index, size, sign):
    re, im = value
    angle_index = angle_index % size
    if angle_index == 0:
        return value
    if 4 * angle_index == size:
        return (-im, re) if sign > 0 else (im, -re)
    if 2 * angle_index == size:
        return (-re, -im)
    angle = 2.0 * math.pi * angle_index / size
    cos, sin = math.cos(angle), sign * math.sin(angle)
    if 8 * angle_index == size:
        return ((re - im) * cos, (re + im) * cos) if sign > 0 else ((re + im) * cos, (im - re) * cos)
    return (re * cos - im * sin, re * sin + im * cos)


def add(a, b):
    return (a[0] + b[0], a[1] + b[1])


def sub(a, b):
    return (a[0] - b[0], a[1] - b[1])


def conj(a):
    return (a[0], -a[1])


def complex_dft(values, sign):
    size = len(values)
    if size == 1:
        return values
    even = complex_dft(values[0::2], sign)
    odd = complex_dft(values[1::2], sign)
    odd = [turn(odd[k], k, size, sign) for k in range(size // 2)]
    return [add(even[k], odd[k]) for k in range(size // 2)] + [
        sub(even[k], odd[k]) for k in range(size // 2)
    ]


def real_dft(values):
    size = len(values)
    if size == 2:
        zero = jnp.zeros_like(values[0])
        return [(values[0] + values[1], zero), (values[0] - values[1], zero)]
    even, odd = real_dft(values[0::2]), real_dft(values[1::2])
    half = size // 2
    zero = jnp.zeros_like(values[0])
    result = [None] * (half + 1)
    result[0] = (even[0][0] + odd[0][0], zero)
    result[half] = (even[0][0] - odd[0][0], zero)
    for k in range(1, half // 2 + 1):
        if 2 * k == half:
            result[k] = (even[k][0], -odd[k][0])
        else:
            moved = turn(odd[k], k, size, -1)
            result[k] = add(even[k], moved)
            result[half - k] = conj(sub(even[k], moved))
    return result


def real_inverse(values, size):
    half = size // 2
    if size == 2:
        a, b = values[0][0], values[1][0]
        return [a + b, a - b]
    even, odd = [], []
    for k in range(half // 2 + 1):
        if k == 0:
            even.append((values[0][0] + values[half][0], None))
            odd.append((values[0][0] - values[half][0], None))
        elif 2 * k == half:
            even.append((2.0 * values[k][0], None))
            odd.append((-2.0 * values[k][1], None))
        else:
            other = conj(values[half - k])
            even.append(add(values[k], other))
            odd.append(turn(sub(values[k], other), k, size, 1))
    first, second = real_inverse(even, half), real_inverse(odd, half)
    return [item for both in zip(first, second) for item in both]


def split_dot(x, high_table, low_table):
    high = x.astype(jnp.bfloat16)
    low = (x - high.astype(jnp.float32)).astype(jnp.bfloat16)

    def dot(a, b):
        return jnp.dot(a, b, preferred_element_type=jnp.float32)

    return dot(high, high_table) + (dot(low, high_table) + dot(high, low_table))


def to_sublanes(row, count, start):
    size = row.shape[1]
    row_ids = lax.broadcasted_iota(jnp.int32, (count, size), 0)
    col_ids = lax.broadcasted_iota(jnp.int32, (count, size), 1)
    spread = jnp.broadcast_to(row.astype(jnp.float32), (count, size))
    picked = jnp.where(col_ids == row_ids + start, spread, 0.0)
    return jnp.sum(picked, axis=1, keepdims=True).astype(jnp.int32)


def kernel(
    groups, blocks,
    traces_hbm, *rest,
):
    numbers_hbm, rows_hbm, out, scratch = rest[0], rest[1], rest[2], rest[3:]
    traces, small, scratch = scratch[0], scratch[1:4], scratch[4:]
    numbers, table, twist = small
    small_hbm = (
        numbers_hbm, rows_hbm.at[0 : 2 * LANES], rows_hbm.at[2 * LANES : 2 * LANES + twist.shape[0]],
    )
    ext, second, up, got, spec, table_hi, table_lo = scratch[:7]
    halo_send, halo_recv, part_send, part_recv, load_sem, small_sem = scratch[7:]
    shot_local, chan_local, length = traces.shape
    outer = length // LANES
    half = outer // 2 + 1
    rec = chan_local // groups
    shots = groups * shot_local
    tiles = outer // 8
    back = outer // 4
    span = outer + back
    unit_rows = (chan_local + 2 * HALO) * 8
    halo_rows = HALO * 8
    part = lax.axis_index("shot")
    block = lax.axis_index("chan")
    mesh_id = pl.DeviceIdType.MESH
    has_left = block > 0
    has_right = block < blocks - 1
    left = jnp.maximum(block - 1, 0)
    right = jnp.minimum(block + 1, blocks - 1)
    q_bits = max((length // 4 // LANES - 1).bit_length(), 0)

    small_loads = [
        pltpu.make_async_copy(small_hbm[i], small[i], small_sem.at[i]) for i in range(len(small))
    ]
    trace_loads = [
        pltpu.make_async_copy(traces_hbm.at[s], traces.at[s], load_sem.at[s]) for s in range(shot_local)
    ]
    small_loads[0].start()
    for load in trace_loads + small_loads[1:]:
        load.start()

    barrier = pltpu.get_barrier_semaphore()

    @pl.when(has_left)
    def _():
        pl.semaphore_signal(barrier, inc=1, device_id=(part, left), device_id_type=mesh_id)

    @pl.when(has_right)
    def _():
        pl.semaphore_signal(barrier, inc=1, device_id=(part, right), device_id_type=mesh_id)

    for offset in range(1, groups):
        pl.semaphore_signal(
            barrier, inc=1, device_id=(lax.rem(part + offset, groups), block), device_id_type=mesh_id
        )

    def rotate_index(column, sign, rows):
        lanes = lax.broadcasted_iota(jnp.int32, (rows, LANES), 1)
        low = jnp.broadcast_to(column & (LANES - 1), (rows, LANES))
        if sign > 0:
            place = lanes + low
            return place & (LANES - 1), place >= LANES
        place = lanes - low
        return place & (LANES - 1), place < 0

    def whole_chunks(column, rows):
        return [
            jnp.broadcast_to((column >> (7 + bit)) & 1, (rows, LANES)) == 1 for bit in range(q_bits)
        ]

    def move_earlier(chunks, column, rows):
        index, crossed = rotate_index(column, 1, rows)
        zero = jnp.zeros((rows, LANES), jnp.float32)
        turned = [jnp.take_along_axis(chunk, index, axis=1) for chunk in chunks]

        def at(items, place):
            return items[place] if place < outer else zero

        moved = [jnp.where(crossed, at(turned, a + 1), turned[a]) for a in range(outer)]
        for bit, chosen in enumerate(whole_chunks(column, rows)):
            moved = [jnp.where(chosen, at(moved, a + (1 << bit)), moved[a]) for a in range(outer)]
        return moved

    def move_later(chunks, chosen, index, crossed):
        moved = dict(enumerate(chunks))
        first = back + 8 - len(chunks)
        for bit in reversed(range(q_bits)):
            first += 1 << bit
            moved = {
                a: jnp.where(chosen[bit], moved[a - (1 << bit)], moved[a])
                for a in range(first, back + 8)
            }
        turned = {a: jnp.take_along_axis(moved[a], index, axis=1) for a in range(back - 1, back + 8)}
        return [jnp.where(crossed, turned[a - 1], turned[a]) for a in range(back, back + 8)]

    def halo_copies(unit):
        base = pl.multiple_of(unit * unit_rows, 8)
        to_right = pltpu.make_async_remote_copy(
            src_ref=ext.at[pl.ds(base + chan_local * 8, halo_rows)],
            dst_ref=ext.at[pl.ds(base, halo_rows)],
            send_sem=halo_send.at[unit, 0],
            recv_sem=halo_recv.at[unit, 0],
            device_id=(part, right),
            device_id_type=mesh_id,
        )
        to_left = pltpu.make_async_remote_copy(
            src_ref=ext.at[pl.ds(base + halo_rows, halo_rows)],
            dst_ref=ext.at[pl.ds(base + halo_rows + chan_local * 8, halo_rows)],
            send_sem=halo_send.at[unit, 1],
            recv_sem=halo_recv.at[unit, 1],
            device_id=(part, left),
            device_id_type=mesh_id,
        )
        return to_right, to_left

    def part_copy(s, tile, offset):
        other = lax.rem(part + offset, groups)
        rows = pl.ds(pl.multiple_of(tile * 8, 8), 8)
        return pltpu.make_async_remote_copy(
            src_ref=up.at[s, other, rows],
            dst_ref=got.at[part * shot_local + s, rows],
            send_sem=part_send.at[s * tiles + tile, offset - 1],
            recv_sem=part_recv.at[s * tiles + tile, offset - 1],
            device_id=(other, block),
            device_id_type=mesh_id,
        )

    def align(s):
        row = numbers[pl.ds(s, 1), :]
        for top in range(0, chan_local, 8):
            column = to_sublanes(row, 8, top)
            chunks = [traces[s, top : top + 8, a * LANES : (a + 1) * LANES] for a in range(outer)]
            moved = move_earlier(chunks, column, 8)
            for a in range(outer):
                start = (s * tiles + a // 8) * unit_rows + (HALO + top) * 8 + a % 8
                ext[pl.ds(start, 8, stride=8), :] = moved[a]

    def send_halos(s):
        odd = block % 2 == 1
        for tile in range(tiles):
            to_right, to_left = halo_copies(s * tiles + tile)
            pl.when(has_right & odd)(to_right.start)
            pl.when(has_left & jnp.logical_not(odd))(to_left.start)
        for tile in range(tiles):
            to_right, to_left = halo_copies(s * tiles + tile)
            pl.when(has_right & jnp.logical_not(odd))(to_right.start)
            pl.when(has_left & odd)(to_left.start)

    small_loads[0].wait()
    trace_loads[0].wait()
    align(0)
    expected = has_left.astype(jnp.int32) + has_right.astype(jnp.int32) + (groups - 1)
    pl.semaphore_wait(barrier, expected)
    send_halos(0)

    def align_step(s, carry):
        align(s)
        send_halos(s)
        return carry

    for load in trace_loads[1:]:
        load.wait()
    lax.fori_loop(1, shot_local, align_step, 0)
    for load in small_loads[1:]:
        load.wait()
    table_hi[...] = table[...].astype(jnp.bfloat16)
    table_lo[...] = (table[...] - table_hi[...].astype(jnp.float32)).astype(jnp.bfloat16)

    def clear(first):
        def clear_step(unit, carry):
            rows = pl.ds(pl.multiple_of(unit * unit_rows + first, 8), halo_rows)
            ext[rows, :] = jnp.zeros((halo_rows, LANES), jnp.float32)
            return carry

        lax.fori_loop(0, shot_local * tiles, clear_step, 0)

    pl.when(jnp.logical_not(has_left))(lambda: clear(0))
    pl.when(jnp.logical_not(has_right))(lambda: clear(halo_rows + chan_local * 8))
    for c in range(chan_local):
        second[c * span : c * span + back, :] = jnp.zeros((back, LANES), jnp.float32)

    def forward(load, shot_id):
        values = real_dft([load(a) for a in range(outer)])
        for c in range(half):
            re, im = values[c]
            cos, sin = twist[c : c + 1, 0:LANES], twist[c : c + 1, LANES : 2 * LANES]
            spec[shot_id, c, :, 0:LANES] = re * cos + im * sin
            spec[shot_id, c, :, LANES : 2 * LANES] = im * cos - re * sin
        padded = spec.shape[1]
        if padded > half:
            spec[shot_id, half:padded] = jnp.zeros((padded - half, rec, 2 * LANES), jnp.float32)
        flat = spec[shot_id].reshape(padded * rec, 2 * LANES)
        flat = split_dot(flat, table_hi[...], table_lo[...])
        spec[shot_id] = flat.reshape(padded, rec, 2 * LANES)

    edge_low = jnp.broadcast_to(has_left, (8, LANES))
    edge_high = jnp.broadcast_to(has_right, (8, LANES))

    def drain_parts(s):
        for tile in range(tiles):
            for offset in range(1, groups):
                part_copy(s, tile, offset).wait_send()

    def clean_step(s, carry):
        shot_id = part * shot_local + s
        row = numbers[pl.ds(s, 1), :]
        moves = []
        for g in range(groups):
            column = to_sublanes(row, rec, g * rec)
            low = to_sublanes(numbers[shot_local : shot_local + 1, :], rec, g * rec)
            high = to_sublanes(numbers[shot_local + 1 : shot_local + 2, :], rec, g * rec)
            inside = ((low <= shot_id) & (high > shot_id)).astype(jnp.int32)
            inside = jnp.broadcast_to(inside, (rec, LANES)) == 1
            moves.append((whole_chunks(column, rec),) + rotate_index(column, -1, rec) + (inside,))

        def unit_step(tile, carry):
            unit = s * tiles + tile
            to_right, to_left = halo_copies(unit)
            pl.when(has_left)(to_right.wait_recv)
            pl.when(has_right)(to_left.wait_recv)
            base = unit * unit_rows

            def rows_at(j):
                return ext[pl.ds(pl.multiple_of(base + j * 8, 8), 8), :]

            rows = {j: rows_at(j) for j in range(chan_local + 2 * HALO)}
            centers = list(range(REACH, chan_local + 2 * HALO - REACH))
            found = median_rows(rows, centers)
            cleaned = {}
            for j in centers:
                value = rows[j] - found[j]
                if j < HALO:
                    value = jnp.where(edge_low, value, 0.0)
                elif j >= HALO + chan_local:
                    value = jnp.where(edge_high, value, 0.0)
                cleaned[j] = value
            centers = list(range(HALO, HALO + chan_local))
            found = median_rows(cleaned, centers)
            for j in centers:
                start = pl.multiple_of((j - HALO) * span + back + tile * 8, 8)
                second[pl.ds(start, 8), :] = cleaned[j] - found[j]

            for g in range(groups):
                chosen, index, crossed, inside = moves[g]
                chunks = [
                    second[pl.ds(g * rec * span + tile * 8 + a, rec, stride=span), :]
                    for a in range(back + 8)
                ]
                for a, value in enumerate(move_later(chunks, chosen, index, crossed)):
                    up[s, g, tile * 8 + a] = jnp.where(inside, value, 0.0)
            for offset in range(1, groups):
                part_copy(s, tile, offset).start()
            return carry

        lax.fori_loop(0, tiles, unit_step, 0)
        forward(lambda a: up[s, part, a], shot_id)

        @pl.when(s > 0)
        def _():
            arrive(s - 1)

        return carry

    def arrive(s):
        for offset in range(1, groups):
            for tile in range(tiles):
                part_copy(s, tile, offset).wait_recv()
            source = lax.rem(part + groups - offset, groups)
            shot_id = source * shot_local + s
            forward(lambda a: got[shot_id, a], shot_id)

    lax.fori_loop(0, shot_local, clean_step, 0)

    def drain_step(unit, carry):
        to_right, to_left = halo_copies(unit)
        pl.when(has_right)(to_right.wait_send)
        pl.when(has_left)(to_left.wait_send)
        return carry

    lax.fori_loop(0, shot_local * tiles, drain_step, 0)
    for s in range(shot_local - 1):
        drain_parts(s)
    arrive(shot_local - 1)

    band = jnp.broadcast_to(to_sublanes(numbers[shot_local + 2 : shot_local + 3, :], rec, part * rec), (rec, LANES))
    lane_ids = lax.broadcasted_iota(jnp.int32, (rec, LANES), 1)

    for c in range(half):
        frequency = lane_ids * outer + c
        freq_abs = jnp.minimum(frequency, length - frequency)
        values = [
            (spec[s, c, :, 0:LANES], spec[s, c, :, LANES : 2 * LANES]) for s in range(shots)
        ]
        waves = complex_dft(values, -1)
        kept = []
        for k in range(shots):
            keep = min(k, shots - k) * band <= freq_abs
            kept.append((jnp.where(keep, waves[k][0], 0.0), jnp.where(keep, waves[k][1], 0.0)))
        values = complex_dft(kept, 1)
        for s in range(shots):
            spec[s, c, :, 0:LANES] = values[s][0]
            spec[s, c, :, LANES : 2 * LANES] = -values[s][1]

    padded = spec.shape[1]
    batch = shots // 2
    for first in range(0, shots, batch):
        flat = spec[first : first + batch].reshape(batch * padded * rec, 2 * LANES)
        flat = split_dot(flat, table_hi[...], table_lo[...])
        spec[first : first + batch] = flat.reshape(batch, padded, rec, 2 * LANES)

    def back(s):
        values = []
        for c in range(half):
            re, minus = spec[s, c, :, 0:LANES], spec[s, c, :, LANES : 2 * LANES]
            cos, sin = twist[c : c + 1, 0:LANES], twist[c : c + 1, LANES : 2 * LANES]
            values.append((re * cos + minus * sin, re * sin - minus * cos))
        for a, value in enumerate(real_inverse(values, outer)):
            out[s, :, a * LANES : (a + 1) * LANES] = value

    def back_step(pair, carry):
        back(2 * pair)
        back(2 * pair + 1)
        return carry

    lax.fori_loop(0, shots // 2, back_step, 0)

    drain_parts(shot_local - 1)


def tables(length):
    outer = length // LANES
    ids = np.arange(LANES)
    angles = 2.0 * np.pi * (np.outer(ids, ids) % LANES) / LANES
    cos, sin = np.cos(angles), np.sin(angles)
    table = np.block([[cos, -sin], [sin, cos]]).astype(np.float32)
    half = outer // 2 + 1
    angles = 2.0 * np.pi * (np.outer(np.arange(half), ids) % length) / length
    rows = np.zeros((16 * 2 * LANES, 2 * LANES), np.float32)
    rows[: 2 * LANES] = table
    rows[2 * LANES : 2 * LANES + half] = np.concatenate([np.cos(angles), np.sin(angles)], axis=1)
    return rows


def local(groups, blocks, traces, shifts, aperture_lo, aperture_hi, dip_band):
    shot_local, chan_local, length = traces.shape
    outer = length // LANES
    rec = chan_local // groups
    shots = groups * shot_local
    padded = outer // 2 + 2
    constants = jnp.asarray(tables(length))
    twist_rows = -(-(outer // 2 + 1) // 8) * 8
    numbers = jnp.concatenate(
        [shifts, aperture_lo[None, :], aperture_hi[None, :], dip_band[None, :]], axis=0
    )
    operands = [traces, numbers, constants]
    others = max(groups - 1, 1)
    units = shot_local * (outer // 8)
    summed = pl.pallas_call(
        functools.partial(kernel, groups, blocks),
        out_shape=jax.ShapeDtypeStruct((shots, rec, length), jnp.float32),
        in_specs=[pl.BlockSpec(memory_space=pltpu.HBM)] * len(operands),
        out_specs=pl.BlockSpec(memory_space=pltpu.VMEM),
        scratch_shapes=[pltpu.VMEM(item.shape, item.dtype) for item in operands[:-1]] + [
            pltpu.VMEM((2 * LANES, 2 * LANES), jnp.float32),
            pltpu.VMEM((twist_rows, 2 * LANES), jnp.float32),
            pltpu.VMEM((shot_local * (chan_local + 2 * HALO) * outer, LANES), jnp.float32),
            pltpu.VMEM((chan_local * (outer + outer // 4), LANES), jnp.float32),
            pltpu.VMEM((shot_local, groups, outer, rec, LANES), jnp.float32),
            pltpu.VMEM((shots, outer, rec, LANES), jnp.float32),
            pltpu.VMEM((shots, padded, rec, 2 * LANES), jnp.float32),
            pltpu.VMEM((2 * LANES, 2 * LANES), jnp.bfloat16),
            pltpu.VMEM((2 * LANES, 2 * LANES), jnp.bfloat16),
            pltpu.SemaphoreType.DMA((units, 2)),
            pltpu.SemaphoreType.DMA((units, 2)),
            pltpu.SemaphoreType.DMA((units, others)),
            pltpu.SemaphoreType.DMA((units, others)),
            pltpu.SemaphoreType.DMA((shot_local,)),
            pltpu.SemaphoreType.DMA((len(operands),)),
        ],
        compiler_params=pltpu.CompilerParams(
            collective_id=0, has_side_effects=True, vmem_limit_bytes=52 * 1024 * 1024
        ),
    )(*operands)
    return summed * np.float32(1.0 / (shots * length))


def solution(mesh):
    return jax.shard_map(
        functools.partial(local, mesh.shape["shot"], mesh.shape["chan"]),
        mesh=mesh,
        in_specs=(P("shot", "chan", None), P("shot", "chan"), P("chan"), P("chan"), P("chan")),
        out_specs=P(None, ("chan", "shot"), None),
        check_vma=False,
    )
```
